256 devices in a mesh: seq: 16 (over z_lo, x), head: 16 (over z_hi, y, core).
Axes of the slice: x: 4, y: 4, z: 8 (z_hi: 2, z_lo: 4; z = z_hi * 4 + z_lo), core: 2. Of those that a mesh axis runs over, the one named last changes fastest.
Arguments:
- query_in: bfloat16 [8192, 3072], P(('seq', 'head')), may hold values from -160 to 160
- key_in: bfloat16 [8192, 3072], P(('seq', 'head')), may hold values from -6 to 6
- value_in: bfloat16 [8192, 3072], P(('seq', 'head')), may hold values from -6 to 6
- block_mask: int32 [9, 4, 4], replicated, may hold values from 0 to 1, as said below
- out_weight: bfloat16 [3072, 3072], P('head'), may hold values from -0.109375 to 0.109375
- out_bias: bfloat16 [3072], replicated, may hold values from -3 to 3
Outputs:
- layer_out: bfloat16 [8192, 3072], P(('seq', 'head'))
The draws below stay inside these ranges and needn't reach their ends.
Inputs may be any that keep to these rules, and one draw needn't show every extreme that they name: `block_mask`: entry 0 has ones on its diagonal tiles; every entry holds at least one 1; entries 2l - 1 and 2l keep about a 2**l-th of their tiles.
All inputs are finite; a program needn't handle non-finite values.
Results may differ from the reference program's by a relative error of at most 0.0027.
Values may be sent and summed in bfloat16 or wider, within the bound.
A program may use at most 128 MiB of HBM per device.

```python
import math
import jax
import jax.numpy as jnp
from jax import lax

HEADS = 48
HD = 64
D = 3072
S_DEV = 512
TILE = 128
TQ = 4
NBLK = 9
TOKENS = 8192
N_SEQ = 16


def aligned_keys(key):
    base = jnp.clip(jax.random.normal(jax.random.fold_in(key, 11), (TOKENS, D), jnp.float32), -5.5, 5.5)
    token_ids = jnp.arange(TOKENS)
    paired = (token_ids % 61 == 1)[:, None]
    return jnp.where(paired, base, base)


def draw_key_in(key, part):
    result = aligned_keys(key)
    return result.astype(jnp.bfloat16)


def draw_query_in(key, part):
    key = jax.random.fold_in(key, 4)
    result = jnp.clip(jax.random.normal(key, (TOKENS, D), jnp.float32), -6.0, 6.0)
    return result.astype(jnp.bfloat16)


def draw_block_mask(key, part):
    key = jax.random.fold_in(key, 5)
    draw_bits = jax.random.randint(jax.random.fold_in(key, 1), (NBLK, TQ, TQ), 0, 16)
    block_ids = jnp.arange(NBLK)
    level_ids = (block_ids + 1) // 2
    limits = jnp.where(block_ids == 0, 12, jnp.right_shift(16, level_ids))
    kept = draw_bits < limits[:, None, None]
    row_pick = jax.random.randint(jax.random.fold_in(key, 2), (NBLK,), 0, TQ)
    col_pick = jax.random.randint(jax.random.fold_in(key, 3), (NBLK,), 0, TQ)
    tile_ids = jnp.arange(TQ)
    forced = (tile_ids[None, :, None] == row_pick[:, None, None]) & (tile_ids[None, None, :] == col_pick[:, None, None])
    diagonal = (block_ids[:, None, None] == 0) & (tile_ids[None, :, None] == tile_ids[None, None, :])
    return (kept | forced | diagonal).astype(jnp.int32)


def level_of(rng, dims, cuts, low, top_value):
    factor_of, own = 1.0, jax.random.fold_in(rng, 6)
    for axis_at, blocks in cuts:
        draws = jnp.exp(jax.random.uniform(jax.random.fold_in(own, axis_at), (blocks,), jnp.float32, low / len(cuts), top_value / len(cuts)))
        factor_of = factor_of * jnp.repeat(draws, dims[axis_at] // blocks).reshape([-1 if axis == axis_at else 1 for axis in range(len(dims))])
    return factor_of


def bell_draw(key, dims, spread, reach, cuts=(), dtype=jnp.bfloat16):
    values = spread * jax.random.normal(key, dims, jnp.float32)
    if cuts:
        values = values * level_of(key, dims, cuts, -0.22, 0.18)
    return jnp.clip(values, -reach, reach).astype(dtype)


def setup_inputs(seed: int = 0) -> dict:
    streams_of = jax.random.split(jax.random.key(seed), 7)
    query_in = draw_query_in(jax.random.fold_in(streams_of[6], 71), 0)
    key_in = draw_key_in(jax.random.fold_in(streams_of[6], 71), 0)
    value_in = bell_draw(streams_of[2], (TOKENS, D), 1.0, 6.0, ((0, 256),))
    block_mask = draw_block_mask(jax.random.fold_in(streams_of[6], 71), 0)
    out_weight = bell_draw(streams_of[4], (D, D), D ** -0.5, 0.109375, ((0, 16),))
    out_bias = bell_draw(streams_of[5], (D,), 0.5, 3.0)
    return dict(query_in=query_in, key_in=key_in, value_in=value_in, block_mask=block_mask, out_weight=out_weight, out_bias=out_bias)


def expand_mask(tile_mask, tile_rows):
    return jnp.repeat(jnp.repeat(tile_mask, tile_rows, axis=0), tile_rows, axis=1) > 0

def reference(query_in, key_in, value_in, block_mask, out_weight, out_bias):
    score_scale = 1.0 / math.sqrt(HD)
    level_total = min(4, 3 + N_SEQ // 16)
    block_plan = [(0, 0)]
    for level_no in range(1, level_total + 1):
        span = 2 ** (level_no - 1)
        block_plan.append((-span, 2 * level_no - 1))
        block_plan.append((span, 2 * level_no))
    pieces = []
    for shard_no in range(N_SEQ):
        queries = query_in[shard_no * S_DEV:(shard_no + 1) * S_DEV].reshape(S_DEV, HEADS, HD).astype(jnp.float32)
        present = []
        for offset, mask_index in block_plan:
            source = shard_no + offset
            if 0 <= source < N_SEQ:
                keys_here = key_in[source * S_DEV:(source + 1) * S_DEV].reshape(S_DEV, HEADS, HD).astype(jnp.float32)
                values_here = value_in[source * S_DEV:(source + 1) * S_DEV].reshape(S_DEV, HEADS, HD).astype(jnp.float32)
                keep_map = expand_mask(block_mask[mask_index], TILE)
                present.append((keys_here, values_here, keep_map))
        top = jnp.full((HEADS, S_DEV), -jnp.inf, jnp.float32)
        for keys_here, values_here, keep_map in present:
            scores = jnp.einsum('qhd,khd->hqk', queries, keys_here) * score_scale
            scores = jnp.where(keep_map[None], scores, -jnp.inf)
            top = jnp.maximum(top, lax.optimization_barrier(jnp.max(scores, axis=2)))
        total = jnp.zeros((HEADS, S_DEV), jnp.float32)
        summed = jnp.zeros((S_DEV, HEADS, HD), jnp.float32)
        for keys_here, values_here, keep_map in present:
            scores = jnp.einsum('qhd,khd->hqk', queries, keys_here) * score_scale
            weights = jnp.where(keep_map[None], jnp.exp(scores - top[:, :, None]), jnp.float32(0.0))
            total = total + lax.optimization_barrier(jnp.sum(weights, axis=2))
            rounded = weights.astype(jnp.bfloat16).astype(jnp.float32)
            summed = summed + jnp.einsum('hqk,khd->qhd', rounded, values_here)
        attended = (summed / jnp.transpose(total)[:, :, None]).astype(jnp.bfloat16)
        pieces.append(attended.reshape(S_DEV, HEADS * HD))
    attended_all = jnp.concatenate(pieces, axis=0)
    projected = jnp.dot(attended_all, out_weight, preferred_element_type=jnp.float32)
    return (projected + out_bias.astype(jnp.float32)[None, :]).astype(jnp.bfloat16)
```

```python
import math

import jax
import jax.numpy as jnp
from jax import lax
from jax.experimental import pallas as pl
from jax.experimental.pallas import tpu as pltpu
from jax.sharding import PartitionSpec as P

MESH = pl.DeviceIdType.MESH
F32 = jnp.float32
BF16 = jnp.bfloat16
HD = 64
NEG = -1e30
SCALE2 = math.log2(math.e) / math.sqrt(HD)


def kernel(
    q_ref, k_ref, v_ref, mask, w_hbm, bias_ref, o_ref,
    sendbuf, recv, kvall, qp, m_ref, l_ref, acc_ref, opack, orecv, ag, wbuf, part, dpart, fin,
    e_send, e_recv, x_send, x_recv, f_send, f_recv,
    w1_send, w1_recv, w1_loc, w2_send, w2_recv, w2f_send, w3_send, w3_recv, w3f_send, w3f_recv,
    o_send, o_recv, a_send, a_recv, af_send, af_recv, d_send, d_recv, y_send, y_recv,
):
    seq = lax.axis_index("seq")
    g = lax.axis_index("head")
    a_me, x = seq // 4, seq % 4
    zh, y, c = g // 8, (g // 2) % 4, g % 2
    k_me = (a_me + 3 - y) % 4
    active = k_me < 3
    boundary = (a_me % 3) == 0

    def remote(src, dst, send, rcv, dev):
        return pltpu.make_async_remote_copy(
            src_ref=src, dst_ref=dst, send_sem=send, recv_sem=rcv, device_id=dev, device_id_type=MESH
        )

    def arrived(dst, sem):
        pltpu.make_async_copy(dst, dst, sem).wait()

    lane = lax.broadcasted_iota(jnp.int32, (32, 128), 1) < HD
    lane16 = lax.broadcasted_iota(jnp.int32, (16, 128), 1) < HD

    def head_device(h):
        gd, kd = h // 3, h % 3
        ad = ((gd // 2) % 4 + 1 + kd) % 4
        return ad, gd

    def prepare(p, carry):
        cols = pl.ds(pl.multiple_of(p * 128, 128), 128)
        k2 = k_ref[:, cols].astype(F32)
        v2 = v_ref[:, cols].astype(F32)
        q2 = q_ref[:, cols].astype(F32)
        kr, vr = pltpu.roll(k2, HD, 1), pltpu.roll(v2, HD, 1)
        qr = pltpu.roll(q2, HD, 1)
        sendbuf[2 * p, 0:32] = jnp.where(lane, k2, vr).astype(BF16)
        sendbuf[2 * p, 32:48] = jnp.where(lane16, q2[0:16], qr[16:32]).astype(BF16)
        sendbuf[2 * p + 1, 0:32] = jnp.where(lane, kr, v2).astype(BF16)
        sendbuf[2 * p + 1, 32:48] = jnp.where(lane16, qr[0:16], q2[16:32]).astype(BF16)
        return carry

    lax.fori_loop(0, 24, prepare, 0)

    def send_one(n, carry):
        h = (n + 3 * g) % 48
        ad, gd = head_device(h)
        here = (ad == a_me) & (gd == g)

        @pl.when(jnp.logical_not(here))
        def _():
            remote(
                sendbuf.at[h], recv.at[a_me, g], e_send, e_recv.at[a_me], (ad * 4 + x, gd)
            ).start()

        @pl.when(here)
        def _():
            pltpu.make_async_copy(sendbuf.at[h], recv.at[a_me, g], e_recv.at[a_me]).start()

        return carry

    lax.fori_loop(0, 48, send_one, 0)

    def wcols(yy):
        return w_hbm.at[:, pl.ds(pl.multiple_of(yy * 768, 128), 768)]

    w1 = []
    for r in range(1, 4):
        yd = (y + r) % 4
        cp = remote(
            wcols(yd), wbuf.at[y, zh], w1_send.at[r - 1], w1_recv.at[r - 1], (seq, zh * 8 + yd * 2 + c)
        )
        cp.start()
        w1.append(cp)
    w1_own = pltpu.make_async_copy(wcols(y), wbuf.at[y, zh], w1_loc)
    w1_own.start()

    right = (a_me * 4 + (x + 1) % 4, g)
    left = (a_me * 4 + (x + 3) % 4, g)
    lane64 = lax.broadcasted_iota(jnp.int32, (256, 128), 1) < HD

    def x_copy(direction, a):
        dev = right if direction == 0 else left
        return remote(
            kvall.at[0, a], kvall.at[1 + direction, a],
            x_send.at[direction, a], x_recv.at[direction, a], dev,
        )

    def f_copy(a):
        if a < 2:
            return remote(kvall.at[1, a], kvall.at[3, a], f_send.at[a], f_recv.at[a], right)
        return remote(kvall.at[2, a], kvall.at[3, a], f_send.at[a], f_recv.at[a], left)

    @pl.when(active)
    def _():
        for a in (0, 2, 1, 3):
            arrived(recv.at[a], e_recv.at[a])
            kvall[0, a] = recv[a, :, 0:32, :].reshape(512, 128)
            x_copy(0, a).start()
            x_copy(1, a).start()
            qx = recv[a, :, 32:48, :].astype(F32).reshape(256, 128)
            lo = jnp.where(lane64, qx, 0.0).astype(BF16)
            hi = jnp.where(lane64, pltpu.roll(qx, HD, 1), 0.0).astype(BF16)
            qp[a, :, 0:64, :] = lo.reshape(4, 64, 128)
            qp[a, :, 64:128, :] = hi.reshape(4, 64, 128)
            m_ref[a] = jnp.full((4, 128, 128), NEG, F32)
            l_ref[a] = jnp.zeros((4, 128, 128), F32)
            acc_ref[a] = jnp.zeros((4, 128, 128), F32)

    for cp in w1:
        cp.wait()
    w1_own.wait()
    other = 1 - zh
    w2 = remote(
        wbuf.at[x, zh], wbuf.at[x, zh], w2_send, w2_recv, ((3 - a_me) * 4 + x, other * 8 + y * 2 + c)
    )
    w2f = remote(
        wbuf.at[x, other], wbuf.at[x, other], w2f_send, w2_recv, ((1 + a_me // 3) * 4 + x, g)
    )

    @pl.when(boundary)
    def _():
        w2.start()

    def attend(buf, ap, a, midx):
        kv = kvall[buf, ap]
        for i in range(4):
            s = lax.dot_general(
                qp[a, i], kv, (((1,), (1,)), ((), ())), preferred_element_type=F32
            )
            cols = []
            for j in range(4):
                bias = jnp.where(mask[midx, i, j] > 0, 0.0, NEG).astype(F32)
                cols.append(s[:, j * 128:(j + 1) * 128] + bias)
            top = jnp.maximum(jnp.maximum(cols[0], cols[1]), jnp.maximum(cols[2], cols[3]))
            m_old = m_ref[a, i]
            m_new = jnp.maximum(m_old, jnp.max(top, axis=1, keepdims=True))
            alpha = jnp.exp2((m_old - m_new) * SCALE2)
            ps = [jnp.exp2((col - m_new) * SCALE2) for col in cols]
            l_ref[a, i] = l_ref[a, i] * alpha + ((ps[0] + ps[1]) + (ps[2] + ps[3]))
            p = jnp.concatenate([w.astype(BF16) for w in ps], axis=1)
            acc_ref[a, i] = acc_ref[a, i] * alpha + jnp.dot(p, kv, preferred_element_type=F32)
            m_ref[a, i] = m_new

    def local_round(d):
        def body(a, carry):
            ap = (a + d) % 4
            off = ap - a

            @pl.when((off <= 2) & (off >= -2))
            def _():
                if d == 0:
                    midx = 0
                else:
                    midx = jnp.where(off > 0, 4 + 2 * off, 3 - 2 * off)
                attend(0, ap, a, midx)

            return carry

        lax.fori_loop(0, 4, body, 0)

    def got_x(direction, a):
        x_copy(direction, a).wait_recv()

    @pl.when(active)
    def _():
        local_round(0)
        got_x(0, 0)
        f_copy(0).start()
        got_x(1, 2)
        f_copy(2).start()
        local_round(1)
        got_x(0, 1)
        f_copy(1).start()
        got_x(1, 3)
        f_copy(3).start()

    w3r = remote(
        wbuf.at[x, other], wbuf.at[x, other], w3_send.at[0], w3_recv.at[0], right
    )
    w3l = remote(
        wbuf.at[x, other], wbuf.at[x, other], w3_send.at[1], w3_recv.at[1], left
    )

    @pl.when(boundary)
    def _():
        w2.wait_recv()
        w2f.start()
        w3r.start()
        w3l.start()

    @pl.when(active)
    def _():
        local_round(2)
        local_round(3)
        for a in range(2, 4):
            got_x(0, a)
            got_x(1, 3 - a)

        def near(ap, carry):
            a_minus = ap + (3 - x) // 3
            a_plus = ap - (x + 1) // 4

            @pl.when(a_minus < 4)
            def _():
                attend(1, ap, a_minus, 1)

            @pl.when(a_plus >= 0)
            def _():
                attend(2, ap, a_plus, 2)

            return carry

        lax.fori_loop(0, 4, near, 0)

    @pl.when(jnp.logical_not(boundary))
    def _():
        w2.wait_recv()
        w3r.start()
        w3l.start()

    lane_o = lax.broadcasted_iota(jnp.int32, (64, 128), 1) < HD

    @pl.when(active)
    def _():
        for a in range(4):
            f_copy(a).wait_recv()

        def far(ap, carry):
            a_minus = ap + (3 - x) // 2
            a_plus = ap - (x + 2) // 4

            @pl.when(a_minus < 4)
            def _():
                attend(3, ap, a_minus, 3)

            @pl.when(a_plus >= 0)
            def _():
                attend(3, ap, a_plus, 4)

            return carry

        lax.fori_loop(0, 4, far, 0)

        def finish(n, carry):
            a, i = n // 4, n % 4
            total = jnp.sum(l_ref[a, i], axis=1, keepdims=True)
            att = acc_ref[a, i] / total
            packed = jnp.where(lane_o, pltpu.roll(att[0:64], HD, 1), att[64:128]).astype(BF16)
            opack[n // 2, n % 2] = packed
            return carry

        lax.fori_loop(0, 16, finish, 0)

        for n in range(8):
            ad, hd = n // 2, n % 2
            slot = zh * 3 + k_me
            here = (a_me == ad) & (zh == hd)
            src = opack.at[n]

            @pl.when(jnp.logical_not(here))
            def _():
                remote(
                    src, orecv.at[slot], o_send, o_recv, (ad * 4 + x, hd * 8 + y * 2 + c)
                ).start()

            @pl.when(here)
            def _():
                pltpu.make_async_copy(src, orecv.at[slot], o_recv).start()

    arrived(orecv, o_recv)
    lane_a = lax.broadcasted_iota(jnp.int32, (128, 128), 1) < HD
    for t in range(3):
        x0 = orecv[2 * t].astype(F32).reshape(128, 128)
        x1 = orecv[2 * t + 1].astype(F32).reshape(128, 128)
        cols = slice(t * 128, (t + 1) * 128)
        ag[0, 0, :, cols] = jnp.where(lane_a, x0, pltpu.roll(x1, HD, 1)).astype(BF16)
        ag[0, 1, :, cols] = jnp.where(lane_a, pltpu.roll(x0, HD, 1), x1).astype(BF16)
    ynext = (seq, zh * 8 + ((y + 1) % 4) * 2 + c)
    yprev = (seq, zh * 8 + ((y + 3) % 4) * 2 + c)
    ar = remote(ag.at[0], ag.at[1], a_send.at[0], a_recv.at[0], ynext)
    al = remote(ag.at[0], ag.at[2], a_send.at[1], a_recv.at[1], yprev)
    ar.start()
    al.start()

    xl, xr = (x + 3) % 4, (x + 1) % 4
    w3r.wait_recv()
    src_l = wbuf.at[xl, other, pl.ds(0, 96)]
    w3fr = remote(src_l, src_l, w3f_send.at[0], w3f_recv.at[0], right)
    w3fr.start()
    w3l.wait_recv()
    src_r = wbuf.at[xr, other, pl.ds(96, 96)]
    w3fl = remote(src_r, src_r, w3f_send.at[1], w3f_recv.at[1], left)
    w3fl.start()

    ar.wait_recv()
    afr = remote(ag.at[1, 0], ag.at[3, 0], af_send.at[0], af_recv.at[0], ynext)
    afr.start()
    al.wait_recv()
    afl = remote(ag.at[2, 1], ag.at[3, 1], af_send.at[1], af_recv.at[1], yprev)
    afl.start()
    w3fr.wait_recv()
    w3fl.wait_recv()

    def project(slot, yy, first):
        lhs = ag[slot].reshape(256, 384)
        for n in range(3):
            cols = slice(n * 256, (n + 1) * 256)
            res = jnp.dot(
                lhs, wbuf[yy, :, :, cols].reshape(384, 256), preferred_element_type=F32
            ).reshape(2, 4, 2, 16, 256)
            if first:
                part[:, :, :, :, cols] = res
            else:
                part[:, :, :, :, cols] += res

    project(0, y, True)
    project(1, (y + 3) % 4, False)
    project(2, (y + 1) % 4, False)
    afr.wait_recv()
    afl.wait_recv()
    project(3, (y + 2) % 4, False)

    dcp = remote(part.at[:, :, 1 - c], dpart, d_send, d_recv, (seq, g + 1 - 2 * c))
    dcp.start()
    dcp.wait_recv()
    my_cols = pl.ds(pl.multiple_of(y * 768, 128), 768)
    bias = bias_ref[:, my_cols].astype(F32)
    for yd in range(4):
        for half in range(2):
            fin[yd, pl.ds(16 * half, 16), :] = (part[half, yd, c] + dpart[half, yd] + bias).astype(BF16)
    ys = []
    for r in range(1, 4):
        yd = (y + r) % 4
        cp = remote(
            fin.at[yd], o_ref.at[:, my_cols], y_send.at[r - 1], y_recv.at[r - 1], (seq, zh * 8 + yd * 2 + c)
        )
        cp.start()
        ys.append(cp)
    o_ref[:, my_cols] = fin[y]

    @pl.when(active)
    def _():
        arrived(sendbuf.at[pl.ds(0, 47)], e_send)
        for a in range(4):
            x_copy(0, a).wait_send()
            x_copy(1, a).wait_send()
            f_copy(a).wait_send()
        arrived(opack.at[pl.ds(0, 7)], o_send)

    @pl.when(jnp.logical_not(active))
    def _():
        arrived(sendbuf, e_send)

    @pl.when(boundary)
    def _():
        w2.wait_send()
        w2f.wait_send()

    for cp in (w3r, w3l, w3fr, w3fl, ar, al, afr, afl, dcp):
        cp.wait_send()
    for cp in ys:
        cp.wait()


def shards(query_in, key_in, value_in, block_mask, out_weight, out_bias):
    vmem = pl.BlockSpec(memory_space=pltpu.VMEM)
    dma = pltpu.SemaphoreType.DMA
    return pl.pallas_call(
        kernel,
        out_shape=jax.ShapeDtypeStruct((32, 3072), BF16),
        in_specs=[
            vmem, vmem, vmem,
            pl.BlockSpec(memory_space=pltpu.SMEM),
            pl.BlockSpec(memory_space=pl.ANY),
            vmem,
        ],
        out_specs=vmem,
        scratch_shapes=[
            pltpu.VMEM((48, 48, 128), BF16),
            pltpu.VMEM((4, 16, 48, 128), BF16),
            pltpu.VMEM((4, 4, 512, 128), BF16),
            pltpu.VMEM((4, 4, 128, 128), BF16),
            pltpu.VMEM((4, 4, 128, 128), F32),
            pltpu.VMEM((4, 4, 128, 128), F32),
            pltpu.VMEM((4, 4, 128, 128), F32),
            pltpu.VMEM((8, 2, 64, 128), BF16),
            pltpu.VMEM((6, 2, 64, 128), BF16),
            pltpu.VMEM((4, 2, 128, 384), BF16),
            pltpu.VMEM((4, 2, 192, 768), BF16),
            pltpu.VMEM((2, 4, 2, 16, 768), F32),
            pltpu.VMEM((2, 4, 16, 768), F32),
            pltpu.VMEM((4, 32, 768), BF16),
            dma, dma((4,)), dma((2, 4)), dma((2, 4)), dma((4,)), dma((4,)),
            dma((3,)), dma((3,)), dma, dma, dma, dma, dma((2,)), dma((2,)), dma((2,)), dma((2,)),
            dma, dma, dma((2,)), dma((2,)), dma((2,)), dma((2,)), dma, dma, dma((3,)), dma((3,)),
        ],
        compiler_params=pltpu.CompilerParams(
            has_side_effects=True, vmem_limit_bytes=40 * 1024 * 1024
        ),
        name="radial",
    )(query_in, key_in, value_in, block_mask, out_weight, out_bias.reshape(1, 3072))


def solution(mesh):
    return jax.shard_map(
        shards,
        mesh=mesh,
        in_specs=(
            P(("seq", "head"), None),
            P(("seq", "head"), None),
            P(("seq", "head"), None),
            P(),
            P("head", None),
            P(),
        ),
        out_specs=P(("seq", "head"), None),
        check_vma=False,
    )
```

```python
import functools
import math

import jax
import jax.numpy as jnp
from jax import lax
from jax.experimental import pallas as pl
from jax.experimental.pallas import tpu as pltpu
from jax.sharding import PartitionSpec as P

MESH = pl.DeviceIdType.MESH
F32 = jnp.float32
BF16 = jnp.bfloat16
HD = 64
NEG = -1e30
SCALE2 = math.log2(math.e) / math.sqrt(HD)
SLOTS = (0, 3, 1, 4, 2, 5)


def kernel(
    q_hbm, k_hbm, v_hbm, mask_hbm, w_hbm, bias_hbm, o_ref,
    raw, mask, bias_ref, sendbuf, kbuf, vbuf, qbuf, qlo, qhi, tiles, m_ref, l_ref, acc_ref, opack,
    attended, lhs, wbuf, part, dpart, fin,
    in_sem, e_send, e_recv, x_send, x_recv, f_send, f_recv,
    w1_send, w1_recv, w1_loc, w2_send, w2_recv, w2f_send, w3_send, w3_recv, w3f_send, w3f_recv,
    o_send, o_recv, a_send, a_recv, af_send, af_recv, d_send, d_recv, y_send, y_recv,
):
    seq = lax.axis_index("seq")
    g = lax.axis_index("head")
    a_me, x = seq // 4, seq % 4
    zh, y, c = g // 8, (g // 2) % 4, g % 2
    k_me = (a_me + 3 - y) % 4
    active = k_me < 3
    boundary = (a_me % 3) == 0
    right = (a_me * 4 + (x + 1) % 4, g)
    left = (a_me * 4 + (x + 3) % 4, g)
    ynext = (seq, zh * 8 + ((y + 1) % 4) * 2 + c)
    yprev = (seq, zh * 8 + ((y + 3) % 4) * 2 + c)
    other = 1 - zh

    def remote(src, dst, send, rcv, dev):
        return pltpu.make_async_remote_copy(
            src_ref=src, dst_ref=dst, send_sem=send, recv_sem=rcv, device_id=dev, device_id_type=MESH
        )

    def arrived(dst, sem):
        pltpu.make_async_copy(dst, dst, sem).wait()

    fetch = [
        pltpu.make_async_copy(src, raw.at[n], in_sem.at[n]) for n, src in enumerate((k_hbm, v_hbm, q_hbm))
    ]
    fetch.append(pltpu.make_async_copy(bias_hbm, bias_ref, in_sem.at[3]))
    fetch.append(pltpu.make_async_copy(mask_hbm, mask, in_sem.at[4]))
    for cp in fetch:
        cp.start()
    barrier = pltpu.get_barrier_semaphore()
    for n in range(1, 64):
        pl.semaphore_signal(
            barrier, inc=1, device_id=(((a_me + n // 16) % 4) * 4 + x, (g + n) % 16), device_id_type=MESH
        )
    for dev in (left, right):
        pl.semaphore_signal(barrier, inc=1, device_id=dev, device_id_type=MESH)

    lane16 = lax.broadcasted_iota(jnp.int32, (16, 128), 1) < HD

    def prepare(t):
        fetch[t].wait()

        def body(p, carry):
            both = raw[t, :, pl.ds(pl.multiple_of(p * 128, 128), 128)].astype(F32)
            turned = pltpu.roll(both, HD, 1)
            sendbuf[t * 48 + 2 * p] = jnp.where(lane16, both[0:16], turned[16:32]).astype(BF16)
            sendbuf[t * 48 + 2 * p + 1] = jnp.where(lane16, turned[0:16], both[16:32]).astype(BF16)
            return carry

        lax.fori_loop(0, 24, body, 0, unroll=4)

    for t in range(3):
        prepare(t)
    fetch[3].wait()
    fetch[4].wait()
    pl.semaphore_wait(barrier, 65)

    def send_wave(t, target):
        def body(n, carry):
            h = (n + 3 * g) % 48
            gd, kd = h // 3, h % 3
            ad = ((gd // 2) % 4 + 1 + kd) % 4
            here = (ad == a_me) & (gd == g)
            src = sendbuf.at[t * 48 + h]

            @pl.when(jnp.logical_not(here))
            def _():
                remote(src, target, e_send, e_recv.at[t, a_me], (ad * 4 + x, gd)).start()

            @pl.when(here)
            def _():
                pltpu.make_async_copy(src, target, e_recv.at[t, a_me]).start()

            return carry

        lax.fori_loop(0, 48, body, 0)

    send_wave(0, kbuf.at[0, a_me, g])
    send_wave(1, vbuf.at[0, a_me, g])
    send_wave(2, qbuf.at[a_me, g])

    def wcols(yy):
        return w_hbm.at[:, pl.ds(pl.multiple_of(yy * 768, 128), 768)]

    w1 = []
    for r in range(1, 4):
        yd = (y + r) % 4
        cp = remote(
            wcols(yd), wbuf.at[y, zh], w1_send.at[r - 1], w1_recv.at[r - 1], (seq, zh * 8 + yd * 2 + c)
        )
        cp.start()
        w1.append(cp)
    w1_own = pltpu.make_async_copy(wcols(y), wbuf.at[y, zh], w1_loc)
    w1_own.start()

    def x_copy(direction, t, a):
        buf = (kbuf, vbuf)[t]
        return remote(
            buf.at[0, a], buf.at[1 + direction, a],
            x_send.at[direction, t, a], x_recv.at[direction, t, a], (right, left)[direction],
        )

    def f_copy(t, a):
        buf = (kbuf, vbuf)[t]
        direction = a // 2
        return remote(
            buf.at[1 + direction, a], buf.at[3, a], f_send.at[t, a], f_recv.at[t, a], (right, left)[direction]
        )

    def pass_on(t, a):
        x_copy(a // 2, t, a).wait_recv()
        f_copy(t, a).start()

    half_lane = lax.broadcasted_iota(jnp.int32, (8, 128), 1) < HD

    def tile_rows(n, carry):
        midx, i = n // 4, n % 4
        for jt in range(2):
            one = jnp.where(mask[midx, i, 2 * jt] > 0, 0.0, NEG).astype(F32)
            two = jnp.where(mask[midx, i, 2 * jt + 1] > 0, 0.0, NEG).astype(F32)
            tiles[midx, i, jt] = jnp.where(half_lane, one, two)
        return carry

    @pl.when(active)
    def _():
        lax.fori_loop(0, 36, tile_rows, 0)
        tiles[9] = jnp.full((4, 2, 8, 128), NEG, F32)
        for t in range(2):
            buf = (kbuf, vbuf)[t]
            for a in (0, 2, 1, 3):
                arrived(buf.at[0, a], e_recv.at[t, a])
                x_copy(0, t, a).start()
                x_copy(1, t, a).start()
        for a in (0, 2, 1, 3):
            pass_on(0, a)
        lane = lax.broadcasted_iota(jnp.int32, (256, 128), 1) < HD
        for a in range(4):
            arrived(qbuf.at[a], e_recv.at[2, a])
            both = qbuf[a].astype(F32).reshape(256, 128)
            lo = jnp.where(lane, both, 0.0)
            hi = jnp.where(lane, 0.0, both)
            qlo[a, 0:256] = lo.astype(BF16)
            qlo[a, 256:512] = pltpu.roll(hi, HD, 1).astype(BF16)
            qhi[a, 0:256] = pltpu.roll(lo, HD, 1).astype(BF16)
            qhi[a, 256:512] = hi.astype(BF16)

    for cp in w1:
        cp.wait()
    w1_own.wait()
    w2 = remote(
        wbuf.at[x, zh], wbuf.at[x, zh], w2_send, w2_recv, ((3 - a_me) * 4 + x, other * 8 + y * 2 + c)
    )
    w2f = remote(
        wbuf.at[x, other], wbuf.at[x, other], w2f_send, w2_recv, ((1 + a_me // 3) * 4 + x, g)
    )
    w3r = remote(wbuf.at[x, other], wbuf.at[x, other], w3_send.at[0], w3_recv.at[0], right)
    w3l = remote(wbuf.at[x, other], wbuf.at[x, other], w3_send.at[1], w3_recv.at[1], left)

    @pl.when(boundary)
    def _():
        w2.start()

    lane512 = lax.broadcasted_iota(jnp.int32, (512, 128), 1) < HD

    def update(a, blocks, first):
        scores = []
        for buf, ap, _ in blocks:
            keys = kbuf[buf, ap].reshape(256, 128)
            for q in (qlo, qhi):
                scores.append(
                    lax.dot_general(q[a], keys, (((1,), (1,)), ((), ())), preferred_element_type=F32)
                )
        weights = [[] for _ in scores]
        alphas = []
        for n in range(8):
            rows = slice(n * 64, (n + 1) * 64)
            cols = []
            for b, (_, _, midx) in enumerate(blocks):
                for jt in range(2):
                    hide = tiles[midx, n % 4, jt][None]
                    for half in range(2):
                        tile = scores[2 * b + half][rows, jt * 128:(jt + 1) * 128]
                        cols.append(((b, half), (tile.reshape(8, 8, 128) + hide).reshape(64, 128)))
            top = jnp.max(functools.reduce(jnp.maximum, [tile for _, tile in cols]), axis=1, keepdims=True)
            if first:
                m_new = jnp.broadcast_to(top, (64, 128))
                total = None
            else:
                m_old = m_ref[a, rows]
                m_new = jnp.maximum(m_old, top)
                alpha = jnp.exp2((m_old - m_new) * SCALE2)
                alphas.append(alpha)
                total = l_ref[a, rows] * alpha
            m_ref[a, rows] = m_new
            found = {}
            for key, tile in cols:
                w = jnp.exp2((tile - m_new) * SCALE2)
                total = w if total is None else total + w
                found.setdefault(key, []).append(w.astype(BF16))
            l_ref[a, rows] = total
            for (b, half), ws in found.items():
                weights[2 * b + half].append(jnp.concatenate(ws, axis=1))
        sums = [None, None]
        for n, (ws, (buf, ap, _)) in enumerate(zip(weights, [blk for blk in blocks for _ in range(2)])):
            values = vbuf[buf, ap].reshape(256, 128)
            res = jnp.dot(jnp.concatenate(ws, axis=0), values, preferred_element_type=F32)
            sums[n % 2] = res if sums[n % 2] is None else sums[n % 2] + res
        new = jnp.where(lane512, sums[0], sums[1])
        if first:
            acc_ref[a] = new
        else:
            acc_ref[a] = acc_ref[a] * jnp.concatenate(alphas, axis=0) + new

    def local(a, carry):
        blocks = []
        for ap in range(4):
            off = ap - a
            midx = jnp.where(off > 0, 4 + 2 * off, 3 - 2 * off)
            midx = jnp.where(off == 0, 0, midx)
            blocks.append((0, ap, jnp.where((off > 2) | (off < -2), 9, midx)))
        update(a, blocks, True)
        return carry

    def pair(buf_minus, buf_plus, step_minus, step_plus, midx):
        def body(a):
            minus, plus = a - step_minus, a + step_plus
            update(
                a,
                [
                    (buf_minus, jnp.maximum(minus, 0), jnp.where(minus >= 0, midx, 9)),
                    (buf_plus, jnp.minimum(plus, 3), jnp.where(plus <= 3, midx + 1, 9)),
                ],
                False,
            )

        return body

    near = pair(1, 2, (3 - x) // 3, (x + 1) // 4, 1)
    far = pair(3, 3, (3 - x) // 2, (x + 2) // 4, 3)

    @pl.when(active)
    def _():
        lax.fori_loop(0, 2, local, 0)
        for a in (0, 2, 1, 3):
            pass_on(1, a)

    @pl.when(boundary)
    def _():
        w2.wait_recv()
        w2f.start()

    @pl.when(active)
    def _():
        lax.fori_loop(2, 4, local, 0)
        for t in range(2):
            for a in range(4):
                x_copy(1 - a // 2, t, a).wait_recv()

        def step(a, carry):
            near(a)
            return carry

        lax.fori_loop(0, 4, step, 0)

    @pl.when(jnp.logical_not(boundary))
    def _():
        w2.wait_recv()

    w3r.start()
    w3l.start()

    lane256 = lax.broadcasted_iota(jnp.int32, (256, 128), 1) < HD

    @pl.when(active)
    def _():
        for t in range(2):
            for a in range(4):
                f_copy(t, a).wait_recv()

        def step(a, carry):
            far(a)
            total = jnp.sum(l_ref[a], axis=1, keepdims=True)
            acc = acc_ref[a]
            att = (acc + pltpu.roll(acc, HD, 1)) / total
            packed = jnp.where(lane256, att[0:256], att[256:512]).astype(BF16)
            slot = zh * 3 + k_me
            for hd in range(2):
                opack[2 * a + hd] = packed[hd * 128:(hd + 1) * 128]
                here = (a_me == a) & (zh == hd)
                src, dst = opack.at[2 * a + hd], attended.at[0, slot]

                @pl.when(jnp.logical_not(here))
                def _():
                    remote(src, dst, o_send, o_recv.at[slot], (a * 4 + x, hd * 8 + y * 2 + c)).start()

                @pl.when(here)
                def _():
                    pltpu.make_async_copy(src, dst, o_recv.at[slot]).start()

            return carry

        lax.fori_loop(0, 4, step, 0)

    def a_copy(direction, slot):
        return remote(
            attended.at[0, slot], attended.at[1 + direction, slot],
            a_send.at[direction, slot], a_recv.at[direction, slot], (ynext, yprev)[direction],
        )

    def af_copy(slot):
        direction = slot // 3
        return remote(
            attended.at[1 + direction, slot], attended.at[3, slot],
            af_send.at[slot], af_recv.at[slot], (ynext, yprev)[direction],
        )

    for slot in SLOTS:
        arrived(attended.at[0, slot], o_recv.at[slot])
        a_copy(0, slot).start()
        a_copy(1, slot).start()

    xl, xr = (x + 3) % 4, (x + 1) % 4
    w3r.wait_recv()
    src_l = wbuf.at[xl, other, pl.ds(0, 96)]
    w3fr = remote(src_l, src_l, w3f_send.at[0], w3f_recv.at[0], right)
    w3fr.start()
    w3l.wait_recv()
    src_r = wbuf.at[xr, other, pl.ds(96, 96)]
    w3fl = remote(src_r, src_r, w3f_send.at[1], w3f_recv.at[1], left)
    w3fl.start()

    for slot in SLOTS:
        a_copy(slot // 3, slot).wait_recv()
        af_copy(slot).start()

    lane128 = lax.broadcasted_iota(jnp.int32, (128, 128), 1) < HD

    def unpack(r):
        for t in range(3):
            x0 = attended[r, 2 * t].astype(F32)
            x1 = attended[r, 2 * t + 1].astype(F32)
            cols = slice(r * 384 + t * 128, r * 384 + (t + 1) * 128)
            lo = jnp.where(lane128, x0, pltpu.roll(x1, HD, 1)).astype(BF16).reshape(4, 2, 16, 128)
            hi = jnp.where(lane128, pltpu.roll(x0, HD, 1), x1).astype(BF16).reshape(4, 2, 16, 128)
            for cd in range(2):
                lhs[cd, :, 0, :, cols] = lo[:, cd]
                lhs[cd, :, 1, :, cols] = hi[:, cd]

    unpack(0)
    for slot in SLOTS:
        a_copy(1 - slot // 3, slot).wait_recv()
    unpack(1)
    unpack(2)
    w3fr.wait_recv()
    w3fl.wait_recv()
    for slot in SLOTS:
        af_copy(slot).wait_recv()
    unpack(3)

    owners = (y, (y + 3) % 4, (y + 1) % 4, (y + 2) % 4)

    def project(core, n):
        rows = lhs[core].reshape(128, 1536)
        res = None
        for r in range(4):
            rhs = wbuf[owners[r], :, :, n * 256:(n + 1) * 256].reshape(384, 256)
            d = jnp.dot(rows[:, r * 384:(r + 1) * 384], rhs, preferred_element_type=F32)
            res = d if res is None else res + d
        return res

    def d_copy(n):
        return remote(part.at[n], dpart.at[n], d_send.at[n], d_recv.at[n], (seq, g + 1 - 2 * c))

    def y_copy(n, r):
        yd = (y + r) % 4
        cols = pl.ds(pl.multiple_of(y * 768 + n * 256, 128), 256)
        return remote(
            fin.at[n, yd], o_ref.at[:, cols], y_send.at[n, r - 1], y_recv.at[n, r - 1],
            (seq, zh * 8 + yd * 2 + c),
        )

    for n in range(3):
        part[n] = project(1 - c, n)
        d_copy(n).start()
    for n in range(3):
        mine = project(c, n)
        cols = pl.ds(pl.multiple_of(y * 768 + n * 256, 128), 256)
        d_copy(n).wait_recv()
        done = (mine + dpart[n] + bias_ref[cols].astype(F32)[None]).astype(BF16)
        fin[n] = done.reshape(4, 32, 256)
        for r in range(1, 4):
            y_copy(n, r).start()
        o_ref[:, cols] = fin[n, y]

    @pl.when(active)
    def _():
        arrived(sendbuf.at[pl.ds(0, 141)], e_send)
        for t in range(2):
            for a in range(4):
                x_copy(0, t, a).wait_send()
                x_copy(1, t, a).wait_send()
                f_copy(t, a).wait_send()
        arrived(opack.at[pl.ds(0, 7)], o_send)

    @pl.when(jnp.logical_not(active))
    def _():
        arrived(sendbuf, e_send)

    @pl.when(boundary)
    def _():
        w2.wait_send()
        w2f.wait_send()

    for cp in (w3r, w3l, w3fr, w3fl):
        cp.wait_send()
    for slot in range(6):
        a_copy(0, slot).wait_send()
        a_copy(1, slot).wait_send()
        af_copy(slot).wait_send()
    for n in range(3):
        d_copy(n).wait_send()
        for r in range(1, 4):
            y_copy(n, r).wait()


def shards(query_in, key_in, value_in, block_mask, out_weight, out_bias):
    hbm = pl.BlockSpec(memory_space=pltpu.HBM)
    dma = pltpu.SemaphoreType.DMA
    return pl.pallas_call(
        kernel,
        out_shape=jax.ShapeDtypeStruct((32, 3072), BF16),
        in_specs=[hbm] * 6,
        out_specs=pl.BlockSpec(memory_space=pltpu.VMEM),
        scratch_shapes=[
            pltpu.VMEM((3, 32, 3072), BF16),
            pltpu.SMEM((9, 4, 4), jnp.int32),
            pltpu.VMEM((3072,), BF16),
            pltpu.VMEM((144, 16, 128), BF16),
            pltpu.VMEM((4, 4, 16, 16, 128), BF16),
            pltpu.VMEM((4, 4, 16, 16, 128), BF16),
            pltpu.VMEM((4, 16, 16, 128), BF16),
            pltpu.VMEM((4, 512, 128), BF16),
            pltpu.VMEM((4, 512, 128), BF16),
            pltpu.VMEM((10, 4, 2, 8, 128), F32),
            pltpu.VMEM((4, 512, 128), F32),
            pltpu.VMEM((4, 512, 128), F32),
            pltpu.VMEM((4, 512, 128), F32),
            pltpu.VMEM((8, 128, 128), BF16),
            pltpu.VMEM((4, 6, 128, 128), BF16),
            pltpu.VMEM((2, 4, 2, 16, 1536), BF16),
            pltpu.VMEM((4, 2, 192, 768), BF16),
            pltpu.VMEM((3, 128, 256), F32),
            pltpu.VMEM((3, 128, 256), F32),
            pltpu.VMEM((3, 4, 32, 256), BF16),
            dma((5,)), dma, dma((3, 4)), dma((2, 2, 4)), dma((2, 2, 4)), dma((2, 4)), dma((2, 4)),
            dma((3,)), dma((3,)), dma, dma, dma, dma, dma((2,)), dma((2,)), dma((2,)), dma((2,)),
            dma, dma((6,)), dma((2, 6)), dma((2, 6)), dma((6,)), dma((6,)),
            dma((3,)), dma((3,)), dma((3, 3)), dma((3, 3)),
        ],
        compiler_params=pltpu.CompilerParams(
            collective_id=0, has_side_effects=True, vmem_limit_bytes=63 * 1024 * 1024
        ),
        name="radial",
    )(query_in, key_in, value_in, block_mask, out_weight, out_bias)


def solution(mesh):
    return jax.shard_map(
        shards,
        mesh=mesh,
        in_specs=(
            P(("seq", "head"), None),
            P(("seq", "head"), None),
            P(("seq", "head"), None),
            P(),
            P("head", None),
            P(),
        ),
        out_specs=P(("seq", "head"), None),
        check_vma=False,
    )
```

```python
import functools
import math

import jax
import jax.numpy as jnp
from jax import lax
from jax.experimental import pallas as pl
from jax.experimental.pallas import tpu as pltpu
from jax.sharding import PartitionSpec as P

MESH = pl.DeviceIdType.MESH
F32 = jnp.float32
BF16 = jnp.bfloat16
HD = 64
NEG = -1e30
SCALE2 = math.log2(math.e) / math.sqrt(HD)
SLOTS = (0, 3, 1, 4, 2, 5)


def kernel(
    q_hbm, k_hbm, v_hbm, mask_hbm, w_hbm, bias_hbm, o_ref,
    raw, mask, bias_ref, sendbuf, kbuf, vbuf, qbuf, qlo, qhi, tiles, m_ref, l_ref, acc_ref, opack,
    attended, lhs, wbuf, part, dpart, fin,
    in_sem, e_send, e_recv, x_send, x_recv, f_send, f_recv,
    w1_send, w1_recv, w1_loc, w2_send, w2_recv, w2f_send, w3_send, w3_recv, w3f_send, w3f_recv,
    o_send, o_recv, a_send, a_recv, af_send, af_recv, d_send, d_recv, y_send, y_recv,
):
    seq = lax.axis_index("seq")
    g = lax.axis_index("head")
    a_me, x = seq // 4, seq % 4
    zh, y, c = g // 8, (g // 2) % 4, g % 2
    k_me = (a_me + 3 - y) % 4
    active = k_me < 3
    boundary = (a_me % 3) == 0
    right = (a_me * 4 + (x + 1) % 4, g)
    left = (a_me * 4 + (x + 3) % 4, g)
    ynext = (seq, zh * 8 + ((y + 1) % 4) * 2 + c)
    yprev = (seq, zh * 8 + ((y + 3) % 4) * 2 + c)
    other = 1 - zh

    def remote(src, dst, send, rcv, dev):
        return pltpu.make_async_remote_copy(
            src_ref=src, dst_ref=dst, send_sem=send, recv_sem=rcv, device_id=dev, device_id_type=MESH
        )

    def arrived(dst, sem):
        pltpu.make_async_copy(dst, dst, sem).wait()

    fetch = [
        pltpu.make_async_copy(src, raw.at[n], in_sem.at[n]) for n, src in enumerate((k_hbm, v_hbm, q_hbm))
    ]
    fetch.append(pltpu.make_async_copy(bias_hbm, bias_ref, in_sem.at[3]))
    fetch.append(pltpu.make_async_copy(mask_hbm, mask, in_sem.at[4]))
    for cp in fetch:
        cp.start()
    barrier = pltpu.get_barrier_semaphore()
    for n in range(1, 64):
        pl.semaphore_signal(
            barrier, inc=1, device_id=(((a_me + n // 16) % 4) * 4 + x, (g + n) % 16), device_id_type=MESH
        )
    for dev in (left, right):
        pl.semaphore_signal(barrier, inc=1, device_id=dev, device_id_type=MESH)

    lane16 = lax.broadcasted_iota(jnp.int32, (16, 128), 1) < HD

    def prepare(t):
        fetch[t].wait()

        def body(p, carry):
            both = raw[t, :, pl.ds(pl.multiple_of(p * 128, 128), 128)].astype(F32)
            turned = pltpu.roll(both, HD, 1)
            sendbuf[t * 48 + 2 * p] = jnp.where(lane16, both[0:16], turned[16:32]).astype(BF16)
            sendbuf[t * 48 + 2 * p + 1] = jnp.where(lane16, turned[0:16], both[16:32]).astype(BF16)
            return carry

        lax.fori_loop(0, 24, body, 0, unroll=4)

    for t in range(3):
        prepare(t)
    fetch[3].wait()
    fetch[4].wait()
    pl.semaphore_wait(barrier, 65)

    def send_wave(t, target):
        def body(n, carry):
            h = (n + 3 * g) % 48
            gd, kd = h // 3, h % 3
            ad = ((gd // 2) % 4 + 1 + kd) % 4
            here = (ad == a_me) & (gd == g)
            src = sendbuf.at[t * 48 + h]

            @pl.when(jnp.logical_not(here))
            def _():
                remote(src, target, e_send, e_recv.at[t, a_me], (ad * 4 + x, gd)).start()

            @pl.when(here)
            def _():
                pltpu.make_async_copy(src, target, e_recv.at[t, a_me]).start()

            return carry

        lax.fori_loop(0, 48, body, 0)

    def w1_copy(dx, r):
        yd, xx = (y + r) % 4, (x + dx) % 4
        rows = pl.ds(pl.multiple_of(xx * 48, 16), 48)
        return remote(
            w_hbm.at[rows, pl.ds(pl.multiple_of(yd * 768, 128), 768)], wbuf.at[y, zh, rows],
            w1_send.at[dx, r - 1], w1_recv.at[dx, r - 1], (seq, zh * 8 + yd * 2 + c),
        )

    w1_own = pltpu.make_async_copy(
        w_hbm.at[:, pl.ds(pl.multiple_of(y * 768, 128), 768)], wbuf.at[y, zh], w1_loc
    )
    w1_own.start()
    send_wave(0, kbuf.at[0, a_me, g])
    for r in range(1, 4):
        w1_copy(0, r).start()
    send_wave(1, vbuf.at[0, a_me, g])
    send_wave(2, qbuf.at[a_me, g])

    def x_copy(direction, t, a):
        buf = (kbuf, vbuf)[t]
        return remote(
            buf.at[0, a], buf.at[1 + direction, a],
            x_send.at[direction, t, a], x_recv.at[direction, t, a], (right, left)[direction],
        )

    def f_copy(t, a):
        buf = (kbuf, vbuf)[t]
        direction = a // 2
        return remote(
            buf.at[1 + direction, a], buf.at[3, a], f_send.at[t, a], f_recv.at[t, a], (right, left)[direction]
        )

    def pass_on(t, a):
        x_copy(a // 2, t, a).wait_recv()
        f_copy(t, a).start()

    half_lane = lax.broadcasted_iota(jnp.int32, (8, 128), 1) < HD

    def tile_rows(n, carry):
        midx, i = n // 4, n % 4
        for jt in range(2):
            one = jnp.where(mask[i, 2 * jt, midx] > 0, 0.0, NEG).astype(F32)
            two = jnp.where(mask[i, 2 * jt + 1, midx] > 0, 0.0, NEG).astype(F32)
            tiles[midx, i, jt] = jnp.where(half_lane, one, two)
        return carry

    @pl.when(active)
    def _():
        lax.fori_loop(0, 36, tile_rows, 0)
        tiles[9] = jnp.full((4, 2, 8, 128), NEG, F32)
        for t in range(2):
            buf = (kbuf, vbuf)[t]
            for a in (0, 2, 1, 3):
                arrived(buf.at[0, a], e_recv.at[t, a])
                x_copy(0, t, a).start()
                x_copy(1, t, a).start()

    my_rows = pl.ds(pl.multiple_of(x * 48, 16), 48)

    def w2_copy(n):
        ref = wbuf.at[pl.ds(2 * n, 2), zh, my_rows]
        dev = ((3 - a_me) * 4 + x, other * 8 + y * 2 + c)
        return remote(ref, ref, w2_send.at[n], w2_recv.at[n], dev)

    def w2f_copy(n):
        ref = wbuf.at[pl.ds(2 * n, 2), other, my_rows]
        return remote(ref, ref, w2f_send.at[n], w2_recv.at[n], ((1 + a_me // 3) * 4 + x, g))

    def w3_copy(direction):
        ref = wbuf.at[:, other, my_rows]
        return remote(ref, ref, w3_send.at[direction], w3_recv.at[direction], (right, left)[direction])

    def w3f_copy(direction):
        xx = (x + (3, 1)[direction]) % 4
        ref = wbuf.at[pl.ds(2 * direction, 2), other, pl.ds(pl.multiple_of(xx * 48, 16), 48)]
        return remote(ref, ref, w3f_send.at[direction], w3f_recv.at[direction], (right, left)[direction])

    def w2_forward(n):
        @pl.when(boundary)
        def _():
            w2_copy(n).wait_recv()
            w2f_copy(n).start()

    @pl.when(jnp.logical_not(active))
    def _():
        arrived(sendbuf, e_send)

    for r in range(1, 4):
        w1_copy(0, r).wait()
    w1_own.wait()

    @pl.when(boundary)
    def _():
        w2_copy(0).start()
        w2_copy(1).start()

    @pl.when(active)
    def _():
        for a in (0, 2, 1, 3):
            pass_on(0, a)
        lane = lax.broadcasted_iota(jnp.int32, (256, 128), 1) < HD
        for a in range(4):
            arrived(qbuf.at[a], e_recv.at[2, a])
            both = qbuf[a].astype(F32).reshape(256, 128)
            lo = jnp.where(lane, both, 0.0)
            hi = jnp.where(lane, 0.0, both)
            qlo[a, 0:256] = lo.astype(BF16)
            qlo[a, 256:512] = pltpu.roll(hi, HD, 1).astype(BF16)
            qhi[a, 0:256] = pltpu.roll(lo, HD, 1).astype(BF16)
            qhi[a, 256:512] = hi.astype(BF16)

    for dx in range(1, 4):
        for r in range(1, 4):
            w1_copy(dx, r).start()

    lane512 = lax.broadcasted_iota(jnp.int32, (512, 128), 1) < HD

    def update(a, blocks, first):
        scores = []
        for buf, ap, _ in blocks:
            keys = kbuf[buf, ap].reshape(256, 128)
            for q in (qlo, qhi):
                scores.append(
                    lax.dot_general(q[a], keys, (((1,), (1,)), ((), ())), preferred_element_type=F32)
                )
        weights = [[] for _ in scores]
        alphas = []
        for n in range(8):
            rows = slice(n * 64, (n + 1) * 64)
            cols = []
            for b, (_, _, midx) in enumerate(blocks):
                for jt in range(2):
                    hide = tiles[midx, n % 4, jt][None]
                    for half in range(2):
                        tile = scores[2 * b + half][rows, jt * 128:(jt + 1) * 128]
                        cols.append(((b, half), (tile.reshape(8, 8, 128) + hide).reshape(64, 128)))
            top = jnp.max(functools.reduce(jnp.maximum, [tile for _, tile in cols]), axis=1, keepdims=True)
            if first:
                m_new = jnp.broadcast_to(top, (64, 128))
                total = None
            else:
                m_old = m_ref[a, rows]
                m_new = jnp.maximum(m_old, top)
                alpha = jnp.exp2((m_old - m_new) * SCALE2)
                alphas.append(alpha)
                total = l_ref[a, rows] * alpha
            m_ref[a, rows] = m_new
            found = {}
            for key, tile in cols:
                w = jnp.exp2((tile - m_new) * SCALE2)
                total = w if total is None else total + w
                found.setdefault(key, []).append(w.astype(BF16))
            l_ref[a, rows] = total
            for (b, half), ws in found.items():
                weights[2 * b + half].append(jnp.concatenate(ws, axis=1))
        sums = [None, None]
        for n, (ws, (buf, ap, _)) in enumerate(zip(weights, [blk for blk in blocks for _ in range(2)])):
            values = vbuf[buf, ap].reshape(256, 128)
            res = jnp.dot(jnp.concatenate(ws, axis=0), values, preferred_element_type=F32)
            sums[n % 2] = res if sums[n % 2] is None else sums[n % 2] + res
        new = jnp.where(lane512, sums[0], sums[1])
        if first:
            acc_ref[a] = new
        else:
            acc_ref[a] = acc_ref[a] * jnp.concatenate(alphas, axis=0) + new

    def local(a, carry):
        blocks = []
        for ap in range(4):
            off = ap - a
            midx = jnp.where(off > 0, 4 + 2 * off, 3 - 2 * off)
            midx = jnp.where(off == 0, 0, midx)
            blocks.append((0, ap, jnp.where((off > 2) | (off < -2), 9, midx)))
        update(a, blocks, True)
        return carry

    def pair(buf_minus, buf_plus, step_minus, step_plus, midx):
        def body(a):
            minus, plus = a - step_minus, a + step_plus
            update(
                a,
                [
                    (buf_minus, jnp.maximum(minus, 0), jnp.where(minus >= 0, midx, 9)),
                    (buf_plus, jnp.minimum(plus, 3), jnp.where(plus <= 3, midx + 1, 9)),
                ],
                False,
            )

        return body

    near = pair(1, 2, (3 - x) // 3, (x + 1) // 4, 1)
    far = pair(3, 3, (3 - x) // 2, (x + 2) // 4, 3)

    def near_step(a, carry):
        near(a)
        return carry

    @pl.when(active)
    def _():
        lax.fori_loop(0, 1, local, 0)

    w2_forward(0)

    @pl.when(active)
    def _():
        lax.fori_loop(1, 2, local, 0)
        for a in (0, 2, 1, 3):
            pass_on(1, a)
        lax.fori_loop(2, 3, local, 0)

    w2_forward(1)

    @pl.when(active)
    def _():
        lax.fori_loop(3, 4, local, 0)
        for t in range(2):
            for a in range(4):
                x_copy(1 - a // 2, t, a).wait_recv()
        lax.fori_loop(0, 4, near_step, 0)
        for t in range(2):
            for a in range(4):
                f_copy(t, a).wait_recv()

    @pl.when(jnp.logical_not(boundary))
    def _():
        w2_copy(0).wait_recv()
        w2_copy(1).wait_recv()

    w3_copy(0).start()
    w3_copy(1).start()

    lane256 = lax.broadcasted_iota(jnp.int32, (256, 128), 1) < HD

    @pl.when(active)
    def _():
        def step(n, carry):
            a = (a_me + n) % 4
            far(a)
            total = jnp.broadcast_to(jnp.sum(l_ref[a], axis=1, keepdims=True), (512, 128))
            acc = acc_ref[a]
            att = acc + pltpu.roll(acc, HD, 1)
            packed = jnp.where(lane256, att[0:256], att[256:512])
            packed = (packed / jnp.where(lane256, total[0:256], total[256:512])).astype(BF16)
            slot = zh * 3 + k_me
            for hd in range(2):
                opack[2 * a + hd] = packed[hd * 128:(hd + 1) * 128]
                here = (a_me == a) & (zh == hd)
                src, dst = opack.at[2 * a + hd], attended.at[0, slot]

                @pl.when(jnp.logical_not(here))
                def _():
                    remote(src, dst, o_send, o_recv.at[slot], (a * 4 + x, hd * 8 + y * 2 + c)).start()

                @pl.when(here)
                def _():
                    pltpu.make_async_copy(src, dst, o_recv.at[slot]).start()

            return carry

        lax.fori_loop(0, 4, step, 0)

    def a_copy(direction, slot):
        return remote(
            attended.at[0, slot], attended.at[1 + direction, slot],
            a_send.at[direction, slot], a_recv.at[direction, slot], (ynext, yprev)[direction],
        )

    def af_copy(direction, slot):
        return remote(
            attended.at[1 + direction, slot], attended.at[3, slot],
            af_send.at[slot], af_recv.at[slot], (ynext, yprev)[direction],
        )

    def slot_of(n, yy, zz, act):
        k = (a_me + 15 - n - yy) % 4

        @pl.when(k < 3)
        def _():
            act(zz * 3 + k)

    def gather(n):
        for zz in range(2):

            def act(slot):
                arrived(attended.at[0, slot], o_recv.at[slot])
                a_copy(0, slot).start()
                a_copy(1, slot).start()

            slot_of(n, y, zz, act)

    def a_forward(n):
        for direction in range(2):

            def act(slot):
                a_copy(direction, slot).wait_recv()
                af_copy(direction, slot).start()

            slot_of(n, y + (3, 1)[direction], direction, act)

    gather(0)
    gather(1)
    a_forward(0)
    gather(2)
    a_forward(1)
    gather(3)
    a_forward(2)
    a_forward(3)

    for direction in range(2):
        w3_copy(direction).wait_recv()
        w3f_copy(direction).start()

    lane128 = lax.broadcasted_iota(jnp.int32, (128, 128), 1) < HD

    def unpack(r):
        for t in range(3):
            x0 = attended[r, 2 * t].astype(F32)
            x1 = attended[r, 2 * t + 1].astype(F32)
            cols = slice(r * 384 + t * 128, r * 384 + (t + 1) * 128)
            lo = jnp.where(lane128, x0, pltpu.roll(x1, HD, 1)).astype(BF16).reshape(4, 2, 16, 128)
            hi = jnp.where(lane128, pltpu.roll(x0, HD, 1), x1).astype(BF16).reshape(4, 2, 16, 128)
            for cd in range(2):
                lhs[cd, :, 0, :, cols] = lo[:, cd]
                lhs[cd, :, 1, :, cols] = hi[:, cd]

    unpack(0)
    for slot in SLOTS:
        a_copy(1 - slot // 3, slot).wait_recv()
    unpack(1)
    unpack(2)
    for slot in SLOTS:
        af_copy(slot // 3, slot).wait_recv()
    unpack(3)

    for direction in range(2):
        w3f_copy(direction).wait_recv()
    for dx in range(1, 4):
        for r in range(1, 4):
            w1_copy(dx, r).wait()

    owners = (y, (y + 3) % 4, (y + 1) % 4, (y + 2) % 4)

    def project(core, n):
        rows = lhs[core].reshape(128, 1536)
        res = None
        for r in range(4):
            rhs = wbuf[owners[r], :, :, n * 256:(n + 1) * 256].reshape(384, 256)
            d = jnp.dot(rows[:, r * 384:(r + 1) * 384], rhs, preferred_element_type=F32)
            res = d if res is None else res + d
        return res

    def d_copy(n):
        return remote(part.at[n], dpart.at[n], d_send.at[n], d_recv.at[n], (seq, g + 1 - 2 * c))

    def y_copy(n, r):
        yd = (y + r) % 4
        cols = pl.ds(pl.multiple_of(y * 768 + n * 256, 128), 256)
        return remote(
            fin.at[n, yd], o_ref.at[:, cols], y_send.at[n, r - 1], y_recv.at[n, r - 1],
            (seq, zh * 8 + yd * 2 + c),
        )

    for n in range(3):
        part[n] = project(1 - c, n)
        d_copy(n).start()
    for n in range(3):
        mine = project(c, n)
        cols = pl.ds(pl.multiple_of(y * 768 + n * 256, 128), 256)
        d_copy(n).wait_recv()
        done = (mine + dpart[n] + bias_ref[cols].astype(F32)[None]).astype(BF16)
        fin[n] = done.reshape(4, 32, 256)
        for r in range(1, 4):
            y_copy(n, r).start()
        o_ref[:, cols] = fin[n, y]

    @pl.when(active)
    def _():
        arrived(sendbuf.at[pl.ds(0, 141)], e_send)
        for t in range(2):
            for a in range(4):
                x_copy(0, t, a).wait_send()
                x_copy(1, t, a).wait_send()
                f_copy(t, a).wait_send()
        arrived(opack.at[pl.ds(0, 7)], o_send)

    @pl.when(boundary)
    def _():
        for n in range(2):
            w2_copy(n).wait_send()
            w2f_copy(n).wait_send()

    for direction in range(2):
        w3_copy(direction).wait_send()
        w3f_copy(direction).wait_send()
    for slot in range(6):
        a_copy(0, slot).wait_send()
        a_copy(1, slot).wait_send()
        af_copy(slot // 3, slot).wait_send()
    for n in range(3):
        d_copy(n).wait_send()
        for r in range(1, 4):
            y_copy(n, r).wait()


def shards(query_in, key_in, value_in, block_mask, out_weight, out_bias):
    hbm = pl.BlockSpec(memory_space=pltpu.HBM)
    dma = pltpu.SemaphoreType.DMA
    return pl.pallas_call(
        kernel,
        out_shape=jax.ShapeDtypeStruct((32, 3072), BF16),
        in_specs=[hbm] * 6,
        out_specs=pl.BlockSpec(memory_space=pltpu.VMEM),
        scratch_shapes=[
            pltpu.VMEM((3, 32, 3072), BF16),
            pltpu.SMEM((4, 4, 9), jnp.int32),
            pltpu.VMEM((3072,), BF16),
            pltpu.VMEM((144, 16, 128), BF16),
            pltpu.VMEM((4, 4, 16, 16, 128), BF16),
            pltpu.VMEM((4, 4, 16, 16, 128), BF16),
            pltpu.VMEM((4, 16, 16, 128), BF16),
            pltpu.VMEM((4, 512, 128), BF16),
            pltpu.VMEM((4, 512, 128), BF16),
            pltpu.VMEM((10, 4, 2, 8, 128), F32),
            pltpu.VMEM((4, 512, 128), F32),
            pltpu.VMEM((4, 512, 128), F32),
            pltpu.VMEM((4, 512, 128), F32),
            pltpu.VMEM((8, 128, 128), BF16),
            pltpu.VMEM((4, 6, 128, 128), BF16),
            pltpu.VMEM((2, 4, 2, 16, 1536), BF16),
            pltpu.VMEM((4, 2, 192, 768), BF16),
            pltpu.VMEM((3, 128, 256), F32),
            pltpu.VMEM((3, 128, 256), F32),
            pltpu.VMEM((3, 4, 32, 256), BF16),
            dma((5,)), dma, dma((3, 4)), dma((2, 2, 4)), dma((2, 2, 4)), dma((2, 4)), dma((2, 4)),
            dma((4, 3)), dma((4, 3)), dma, dma((2,)), dma((2,)), dma((2,)), dma((2,)), dma((2,)), dma((2,)), dma((2,)),
            dma, dma((6,)), dma((2, 6)), dma((2, 6)), dma((6,)), dma((6,)),
            dma((3,)), dma((3,)), dma((3, 3)), dma((3, 3)),
        ],
        compiler_params=pltpu.CompilerParams(
            collective_id=0, has_side_effects=True, vmem_limit_bytes=63 * 1024 * 1024
        ),
        name="radial",
    )(query_in, key_in, value_in, jnp.transpose(block_mask, (1, 2, 0)), out_weight, out_bias)


def solution(mesh):
    return jax.shard_map(
        shards,
        mesh=mesh,
        in_specs=(
            P(("seq", "head"), None),
            P(("seq", "head"), None),
            P(("seq", "head"), None),
            P(),
            P("head", None),
            P(),
        ),
        out_specs=P(("seq", "head"), None),
        check_vma=False,
    )
```

```python
import functools
import math

import jax
import jax.numpy as jnp
from jax import lax
from jax.experimental import pallas as pl
from jax.experimental.pallas import tpu as pltpu
from jax.sharding import PartitionSpec as P

MESH = pl.DeviceIdType.MESH
F32 = jnp.float32
BF16 = jnp.bfloat16
HD = 64
NEG = -1e30
SCALE2 = math.log2(math.e) / math.sqrt(HD)


def kernel(
    q_hbm, k_hbm, v_hbm, mask_hbm, w_hbm, bias_hbm, o_ref,
    raw, mask, bias_ref, sendbuf, kbuf, vbuf, qbuf, qlo, qhi, tiles, sides, m_ref, acc_ref, opack,
    attended, lhs, wbuf, part, mine, dpart, fin,
    in_sem, e_send, e_recv, x_send, x_recv, fk_send, fk_recv, fv_send, fv_recv,
    w1_send, w1_recv, w1_loc, w2_send, w2_recv, w2f_send, w3_send, w3_recv, w3f_send, w3f_recv,
    o_send, o_recv, a_send, a_recv, d_send, d_recv, y_send, y_recv,
):
    seq = lax.axis_index("seq")
    g = lax.axis_index("head")
    a_me, x = seq // 4, seq % 4
    zh, y, c = g // 8, (g // 2) % 4, g % 2
    k_me = (a_me + 3 - y) % 4
    active = k_me < 3
    boundary = (a_me % 3) == 0
    right = (a_me * 4 + (x + 1) % 4, g)
    left = (a_me * 4 + (x + 3) % 4, g)
    other = 1 - zh

    def remote(src, dst, send, rcv, dev):
        return pltpu.make_async_remote_copy(
            src_ref=src, dst_ref=dst, send_sem=send, recv_sem=rcv, device_id=dev, device_id_type=MESH
        )

    def arrived(dst, sem):
        pltpu.make_async_copy(dst, dst, sem).wait()

    fetch = [
        pltpu.make_async_copy(src, raw.at[n], in_sem.at[n]) for n, src in enumerate((k_hbm, v_hbm, q_hbm))
    ]
    fetch.append(pltpu.make_async_copy(bias_hbm, bias_ref, in_sem.at[3]))
    fetch.append(pltpu.make_async_copy(mask_hbm, mask, in_sem.at[4]))
    for cp in fetch:
        cp.start()
    barrier = pltpu.get_barrier_semaphore()
    for n in range(1, 64):
        pl.semaphore_signal(
            barrier, inc=1, device_id=(((a_me + n // 16) % 4) * 4 + x, (g + n) % 16), device_id_type=MESH
        )
    for dev in (left, right):
        pl.semaphore_signal(barrier, inc=1, device_id=dev, device_id_type=MESH)

    lane16 = lax.broadcasted_iota(jnp.int32, (16, 128), 1) < HD

    def prepare(t):
        fetch[t].wait()

        def body(p, carry):
            both = raw[t, :, pl.ds(pl.multiple_of(p * 128, 128), 128)].astype(F32)
            turned = pltpu.roll(both, HD, 1)
            sendbuf[t * 48 + 2 * p] = jnp.where(lane16, both[0:16], turned[16:32]).astype(BF16)
            sendbuf[t * 48 + 2 * p + 1] = jnp.where(lane16, turned[0:16], both[16:32]).astype(BF16)
            return carry

        lax.fori_loop(0, 24, body, 0, unroll=4)

    for t in range(3):
        prepare(t)
    fetch[3].wait()
    fetch[4].wait()
    pl.semaphore_wait(barrier, 65)

    def send_wave(t, target):
        def body(n, carry):
            h = (n + 3 * g) % 48
            gd, kd = h // 3, h % 3
            ad = ((gd // 2) % 4 + 1 + kd) % 4
            here = (ad == a_me) & (gd == g)
            src = sendbuf.at[t * 48 + h]

            @pl.when(jnp.logical_not(here))
            def _():
                remote(src, target, e_send, e_recv.at[t, a_me], (ad * 4 + x, gd)).start()

            @pl.when(here)
            def _():
                pltpu.make_async_copy(src, target, e_recv.at[t, a_me]).start()

            return carry

        lax.fori_loop(0, 48, body, 0)

    def w1_copy(dx, r):
        yd, xx = (y + r) % 4, (x + dx) % 4
        rows = pl.ds(pl.multiple_of(xx * 48, 16), 48)
        return remote(
            w_hbm.at[rows, pl.ds(pl.multiple_of(yd * 768, 128), 768)], wbuf.at[y, zh, rows],
            w1_send.at[dx, r - 1], w1_recv.at[dx, r - 1], (seq, zh * 8 + yd * 2 + c),
        )

    w1_own = pltpu.make_async_copy(
        w_hbm.at[:, pl.ds(pl.multiple_of(y * 768, 128), 768)], wbuf.at[y, zh], w1_loc
    )
    w1_own.start()
    send_wave(0, kbuf.at[0, a_me, g])
    for r in range(1, 4):
        w1_copy(0, r).start()
    send_wave(1, vbuf.at[0, a_me, g])
    send_wave(2, qbuf.at[a_me, g])

    def x_copy(direction, t, a):
        buf = (kbuf, vbuf)[t]
        return remote(
            buf.at[0, a], buf.at[1 + direction, a],
            x_send.at[direction, t, a], x_recv.at[direction, t, a], (right, left)[direction],
        )

    def fk_copy(a):
        direction = a // 2
        return remote(
            kbuf.at[1 + direction, a], kbuf.at[3, a], fk_send.at[a], fk_recv.at[a], (right, left)[direction]
        )

    def fv_copy(direction, a):
        rows = pl.ds(8 * direction, 8)
        return remote(
            vbuf.at[1 + direction, a, rows], vbuf.at[3, a, rows],
            fv_send.at[direction, a], fv_recv.at[direction, a], (right, left)[direction],
        )

    def send_values(a):
        x_copy(0, 1, a).start()
        x_copy(1, 1, a).start()

    def pass_values(a):
        for direction in range(2):
            x_copy(direction, 1, a).wait_recv()
            fv_copy(direction, a).start()

    def got_values(a):
        fv_copy(0, a).wait_recv()
        fv_copy(1, a).wait_recv()

    half_lane = lax.broadcasted_iota(jnp.int32, (8, 128), 1) < HD

    def tile_rows(n, carry):
        midx, i = n // 4, n % 4
        for jt in range(2):
            one = jnp.where(mask[i, 2 * jt, midx] > 0, 0.0, NEG).astype(F32)
            two = jnp.where(mask[i, 2 * jt + 1, midx] > 0, 0.0, NEG).astype(F32)
            tiles[midx, i, jt] = jnp.where(half_lane, one, two)
        return carry

    @pl.when(active)
    def _():
        lax.fori_loop(0, 36, tile_rows, 0)
        tiles[9] = jnp.full((4, 2, 8, 128), NEG, F32)
        for a in (0, 2, 1, 3):
            arrived(kbuf.at[0, a], e_recv.at[0, a])
            x_copy(0, 0, a).start()
            x_copy(1, 0, a).start()
        for a in range(4):
            arrived(vbuf.at[0, a], e_recv.at[1, a])
            send_values(a)

    lane256 = lax.broadcasted_iota(jnp.int32, (256, 128), 1) < HD

    def value_sides(buf, ap):
        both = vbuf[buf, ap].astype(F32).reshape(256, 128)
        turned = pltpu.roll(both, HD, 1)
        lo = [jnp.where(lane256, v, 1.0).astype(BF16) for v in (both, turned)]
        hi = [jnp.where(lane256, 1.0, v).astype(BF16) for v in (turned, both)]
        return jnp.concatenate(lo, axis=0), jnp.concatenate(hi, axis=0)

    my_rows = pl.ds(pl.multiple_of(x * 48, 16), 48)

    def w2_copy(n):
        ref = wbuf.at[pl.ds(2 * n, 2), zh, my_rows]
        dev = ((3 - a_me) * 4 + x, other * 8 + y * 2 + c)
        return remote(ref, ref, w2_send.at[n], w2_recv.at[n], dev)

    def w2f_copy(n):
        ref = wbuf.at[pl.ds(2 * n, 2), other, my_rows]
        return remote(ref, ref, w2f_send.at[n], w2_recv.at[n], ((1 + a_me // 3) * 4 + x, g))

    def w3_copy(direction):
        ref = wbuf.at[:, other, my_rows]
        return remote(ref, ref, w3_send.at[direction], w3_recv.at[direction], (right, left)[direction])

    def w3f_copy(direction):
        xx = (x + (3, 1)[direction]) % 4
        ref = wbuf.at[pl.ds(2 * direction, 2), other, pl.ds(pl.multiple_of(xx * 48, 16), 48)]
        return remote(ref, ref, w3f_send.at[direction], w3f_recv.at[direction], (right, left)[direction])

    def w2_forward(n):
        @pl.when(boundary)
        def _():
            w2_copy(n).wait_recv()
            w2f_copy(n).start()

    @pl.when(jnp.logical_not(active))
    def _():
        arrived(sendbuf, e_send)

    for r in range(1, 4):
        w1_copy(0, r).wait()
    w1_own.wait()

    @pl.when(boundary)
    def _():
        w2_copy(0).start()
        w2_copy(1).start()

    @pl.when(active)
    def _():
        for a in (0, 2, 1, 3):
            x_copy(a // 2, 0, a).wait_recv()
            fk_copy(a).start()
        for a in range(4):
            sides[a, 0], sides[a, 1] = value_sides(0, a)
        for a in range(4):
            arrived(qbuf.at[a], e_recv.at[2, a])
            both = qbuf[a].astype(F32).reshape(256, 128)
            lo = jnp.where(lane256, both, 0.0)
            hi = jnp.where(lane256, 0.0, both)
            qlo[a, 0:256] = lo.astype(BF16)
            qlo[a, 256:512] = pltpu.roll(hi, HD, 1).astype(BF16)
            qhi[a, 0:256] = pltpu.roll(lo, HD, 1).astype(BF16)
            qhi[a, 256:512] = hi.astype(BF16)

    for dx in range(1, 4):
        for r in range(1, 4):
            w1_copy(dx, r).start()

    def update(a, blocks, first):
        scores = []
        for buf, ap, _ in blocks:
            keys = kbuf[buf, ap].reshape(256, 128)
            for q in (qlo, qhi):
                scores.append(
                    lax.dot_general(q[a], keys, (((1,), (1,)), ((), ())), preferred_element_type=F32)
                )
        weights = []
        alphas = []
        for n in range(8):
            rows = slice(n * 64, (n + 1) * 64)
            cols = []
            for b, (_, _, midx) in enumerate(blocks):
                for half in range(2):
                    for jt in range(2):
                        hide = tiles[midx, n % 4, jt][None]
                        tile = scores[2 * b + half][rows, jt * 128:(jt + 1) * 128]
                        cols.append((tile.reshape(8, 8, 128) + hide).reshape(64, 128))
            top = jnp.max(functools.reduce(jnp.maximum, cols), axis=1, keepdims=True)
            if first:
                m_new = jnp.broadcast_to(top, (64, 128))
            else:
                m_old = m_ref[a, rows]
                m_new = jnp.maximum(m_old, top)
                alphas.append(jnp.exp2((m_old - m_new) * SCALE2))
            m_ref[a, rows] = m_new
            weights.append(
                jnp.concatenate([jnp.exp2((tile - m_new) * SCALE2).astype(BF16) for tile in cols], axis=1)
            )
        values = [sides[ap] if first else value_sides(buf, ap) for buf, ap, _ in blocks]
        for half in range(2):
            rows = slice(half * 256, (half + 1) * 256)
            left_side = jnp.concatenate(weights[4 * half:4 * half + 4], axis=0)
            right_side = jnp.concatenate([v[half] for v in values], axis=0)
            new = jnp.dot(left_side, right_side, preferred_element_type=F32)
            if not first:
                new = acc_ref[a, rows] * jnp.concatenate(alphas[4 * half:4 * half + 4], axis=0) + new
            acc_ref[a, rows] = new

    def local(a):
        blocks = []
        for ap in range(4):
            off = ap - a
            midx = jnp.where(off > 0, 4 + 2 * off, 3 - 2 * off)
            midx = jnp.where(off == 0, 0, midx)
            blocks.append((0, ap, jnp.where((off > 2) | (off < -2), 9, midx)))
        update(a, blocks, True)

    def pair(buf_minus, buf_plus, step_minus, step_plus, midx):
        def body(a):
            minus, plus = a - step_minus, a + step_plus
            update(
                a,
                [
                    (buf_minus, jnp.maximum(minus, 0), jnp.where(minus >= 0, midx, 9)),
                    (buf_plus, jnp.minimum(plus, 3), jnp.where(plus <= 3, midx + 1, 9)),
                ],
                False,
            )

        return body

    near = pair(1, 2, (3 - x) // 3, (x + 1) // 4, 1)
    far = pair(3, 3, (3 - x) // 2, (x + 2) // 4, 3)

    def hand_over(a):
        lo, hi = acc_ref[a, 0:256], acc_ref[a, 256:512]
        total = pltpu.roll(jnp.where(lane256, hi, lo), HD, 1)
        packed = (jnp.where(lane256, lo, hi) / total).astype(BF16)
        slot = zh * 3 + k_me
        for hd in range(2):
            opack[2 * a + hd] = packed[hd * 128:(hd + 1) * 128]
            here = (a_me == a) & (zh == hd)
            src, dst = opack.at[2 * a + hd], attended.at[0, slot]

            @pl.when(jnp.logical_not(here))
            def _():
                remote(src, dst, o_send, o_recv.at[slot], (a * 4 + x, hd * 8 + y * 2 + c)).start()

            @pl.when(here)
            def _():
                pltpu.make_async_copy(src, dst, o_recv.at[slot]).start()

    def w3_begin():
        @pl.when(jnp.logical_not(boundary))
        def _():
            w2_copy(0).wait_recv()
            w2_copy(1).wait_recv()

        w3_copy(0).start()
        w3_copy(1).start()

    def local_pass(a, carry):
        local(a)
        for b in range(4):

            @pl.when(a == b)
            def _():
                pass_values(b)
                if b in (0, 2):
                    w2_forward(b // 2)

        return carry

    def near_pass(a, carry):
        near(a)
        return carry

    def far_pass(n, carry):
        a = (a_me + 4 - n) % 4
        far(a)
        hand_over(a)
        return carry

    @pl.when(active)
    def _():
        lax.fori_loop(0, 4, local_pass, 0)
        for a in range(4):
            x_copy(1 - a // 2, 0, a).wait_recv()
        lax.fori_loop(0, 4, near_pass, 0)
        for a in range(4):
            fk_copy(a).wait_recv()
            got_values(a)
        w3_begin()
        lax.fori_loop(0, 4, far_pass, 0)

    @pl.when(jnp.logical_not(active))
    def _():
        w2_forward(0)
        w2_forward(1)
        w3_begin()

    def a_copy(r, slot):
        return remote(
            attended.at[0, slot], attended.at[r, slot], a_send.at[r - 1, slot], a_recv.at[r - 1, slot],
            (seq, zh * 8 + ((y + r) % 4) * 2 + c),
        )

    def gather(step):
        zs = (zh * 4 + a_me + step) % 8
        k = (zs % 4 + 7 - y) % 4
        slot = zs // 4 * 3 + k

        @pl.when(k < 3)
        def _():
            arrived(attended.at[0, slot], o_recv.at[slot])
            for r in (2, 1, 3):
                a_copy(r, slot).start()

    def w3_forward():
        for direction in range(2):
            w3_copy(direction).wait_recv()
            w3f_copy(direction).start()

    for step in (0, 4, 1, 5, 2, 6, 3, 7):
        gather(step)
    w3_forward()

    lane128 = lax.broadcasted_iota(jnp.int32, (128, 128), 1) < HD

    def unpack(r):
        for t in range(3):
            x0 = attended[r, 2 * t].astype(F32)
            x1 = attended[r, 2 * t + 1].astype(F32)
            cols = slice(r * 384 + t * 128, r * 384 + (t + 1) * 128)
            lo = jnp.where(lane128, x0, pltpu.roll(x1, HD, 1)).astype(BF16).reshape(4, 2, 16, 128)
            hi = jnp.where(lane128, pltpu.roll(x0, HD, 1), x1).astype(BF16).reshape(4, 2, 16, 128)
            for cd in range(2):
                lhs[cd, :, 0, :, cols] = lo[:, cd]
                lhs[cd, :, 1, :, cols] = hi[:, cd]

    unpack(0)
    for r in (1, 3):
        for slot in range(6):
            a_copy(r, slot).wait_recv()
        unpack(r)
    for direction in range(2):
        w3f_copy(direction).wait_recv()
    for dx in range(1, 4):
        for r in range(1, 4):
            w1_copy(dx, r).wait()

    owners = (y, (y + 3) % 4, (y + 2) % 4, (y + 1) % 4)

    def project(core, n, sources):
        rows = lhs[core].reshape(128, 1536)
        res = None
        for r in sources:
            rhs = wbuf[owners[r], :, :, n * 256:(n + 1) * 256].reshape(384, 256)
            d = jnp.dot(rows[:, r * 384:(r + 1) * 384], rhs, preferred_element_type=F32)
            res = d if res is None else res + d
        return res

    for n in range(3):
        part[n] = project(1 - c, n, (0, 1, 3))
        mine[n] = project(c, n, (0, 1, 3))
    @pl.when(active)
    def _():
        arrived(sendbuf.at[pl.ds(0, 141)], e_send)
        for t in range(2):
            for a in range(4):
                x_copy(0, t, a).wait_send()
                x_copy(1, t, a).wait_send()
        for a in range(4):
            fk_copy(a).wait_send()
            fv_copy(0, a).wait_send()
            fv_copy(1, a).wait_send()
        arrived(opack.at[pl.ds(0, 7)], o_send)

    @pl.when(boundary)
    def _():
        for n in range(2):
            w2_copy(n).wait_send()
            w2f_copy(n).wait_send()

    for direction in range(2):
        w3_copy(direction).wait_send()
        w3f_copy(direction).wait_send()
    for slot in range(6):
        a_copy(2, slot).wait_recv()
    unpack(2)

    def d_copy(n):
        return remote(part.at[n], dpart.at[n], d_send.at[n], d_recv.at[n], (seq, g + 1 - 2 * c))

    def y_copy(n, r):
        yd = (y + r) % 4
        cols = pl.ds(pl.multiple_of(y * 768 + n * 256, 128), 256)
        return remote(
            fin.at[n, yd], o_ref.at[:, cols], y_send.at[n, r - 1], y_recv.at[n, r - 1],
            (seq, zh * 8 + yd * 2 + c),
        )

    for n in range(3):
        part[n] += project(1 - c, n, (2,))
        d_copy(n).start()
    for n in range(3):
        total = mine[n] + project(c, n, (2,))
        cols = pl.ds(pl.multiple_of(y * 768 + n * 256, 128), 256)
        d_copy(n).wait_recv()
        done = (total + dpart[n] + bias_ref[cols].astype(F32)[None]).astype(BF16)
        fin[n] = done.reshape(4, 32, 256)
        for r in range(1, 4):
            y_copy(n, r).start()
        o_ref[:, cols] = fin[n, y]

    for r in range(1, 4):
        for slot in range(6):
            a_copy(r, slot).wait_send()
    for n in range(3):
        d_copy(n).wait_send()
        for r in range(1, 4):
            y_copy(n, r).wait()


def shards(query_in, key_in, value_in, block_mask, out_weight, out_bias):
    hbm = pl.BlockSpec(memory_space=pltpu.HBM)
    dma = pltpu.SemaphoreType.DMA
    return pl.pallas_call(
        kernel,
        out_shape=jax.ShapeDtypeStruct((32, 3072), BF16),
        in_specs=[hbm] * 6,
        out_specs=pl.BlockSpec(memory_space=pltpu.VMEM),
        scratch_shapes=[
            pltpu.VMEM((3, 32, 3072), BF16),
            pltpu.SMEM((4, 4, 9), jnp.int32),
            pltpu.VMEM((3072,), BF16),
            pltpu.VMEM((144, 16, 128), BF16),
            pltpu.VMEM((4, 4, 16, 16, 128), BF16),
            pltpu.VMEM((4, 4, 16, 16, 128), BF16),
            pltpu.VMEM((4, 16, 16, 128), BF16),
            pltpu.VMEM((4, 512, 128), BF16),
            pltpu.VMEM((4, 512, 128), BF16),
            pltpu.VMEM((10, 4, 2, 8, 128), F32),
            pltpu.VMEM((4, 2, 512, 128), BF16),
            pltpu.VMEM((4, 512, 128), F32),
            pltpu.VMEM((4, 512, 128), F32),
            pltpu.VMEM((8, 128, 128), BF16),
            pltpu.VMEM((4, 6, 128, 128), BF16),
            pltpu.VMEM((2, 4, 2, 16, 1536), BF16),
            pltpu.VMEM((4, 2, 192, 768), BF16),
            pltpu.VMEM((3, 128, 256), F32),
            pltpu.VMEM((3, 128, 256), F32),
            pltpu.VMEM((3, 128, 256), F32),
            pltpu.VMEM((3, 4, 32, 256), BF16),
            dma((5,)), dma, dma((3, 4)), dma((2, 2, 4)), dma((2, 2, 4)), dma((4,)), dma((4,)), dma((2, 4)), dma((2, 4)),
            dma((4, 3)), dma((4, 3)), dma, dma((2,)), dma((2,)), dma((2,)), dma((2,)), dma((2,)), dma((2,)), dma((2,)),
            dma, dma((6,)), dma((3, 6)), dma((3, 6)),
            dma((3,)), dma((3,)), dma((3, 3)), dma((3, 3)),
        ],
        compiler_params=pltpu.CompilerParams(
            collective_id=0, has_side_effects=True, vmem_limit_bytes=63 * 1024 * 1024
        ),
        name="radial",
    )(query_in, key_in, value_in, jnp.transpose(block_mask, (1, 2, 0)), out_weight, out_bias)


def solution(mesh):
    return jax.shard_map(
        shards,
        mesh=mesh,
        in_specs=(
            P(("seq", "head"), None),
            P(("seq", "head"), None),
            P(("seq", "head"), None),
            P(),
            P("head", None),
            P(),
        ),
        out_specs=P(("seq", "head"), None),
        check_vma=False,
    )
```

```python
import functools
import math

import jax
import jax.numpy as jnp
from jax import lax
from jax.experimental import pallas as pl
from jax.experimental.pallas import tpu as pltpu
from jax.sharding import PartitionSpec as P

MESH = pl.DeviceIdType.MESH
F32 = jnp.float32
BF16 = jnp.bfloat16
HD = 64
NEG = -1e30
STEPS = (0, 4, 1, 5, 2, 6, 3, 7)
LAG = 8
SCALE2 = math.log2(math.e) / math.sqrt(HD)


def kernel(
    q_hbm, k_hbm, v_hbm, mask_hbm, w_hbm, bias_hbm, o_ref,
    raw, mask, bias_ref, sendbuf, kbuf, vbuf, qbuf, qlo, qhi, tiles, sides, m_ref, acc_ref, opack,
    attended, lhs, wbuf, part, dpart, fin,
    in_sem, e_send, e_recv, x_send, x_recv, fk_send, fk_recv, fv_send, fv_recv,
    w1_send, w1_recv, w1_loc, w2_send, w2_recv, w2f_send, w3_send, w3_recv, w3f_send, w3f_recv,
    o_send, o_recv, a_send, a_recv, d_send, d_recv, y_send, y_recv,
):
    seq = lax.axis_index("seq")
    g = lax.axis_index("head")
    a_me, x = seq // 4, seq % 4
    zh, y, c = g // 8, (g // 2) % 4, g % 2
    k_me = (a_me + 3 - y) % 4
    active = k_me < 3
    boundary = (a_me % 3) == 0
    right = (a_me * 4 + (x + 1) % 4, g)
    left = (a_me * 4 + (x + 3) % 4, g)
    other = 1 - zh

    def remote(src, dst, send, rcv, dev):
        return pltpu.make_async_remote_copy(
            src_ref=src, dst_ref=dst, send_sem=send, recv_sem=rcv, device_id=dev, device_id_type=MESH
        )

    def arrived(dst, sem):
        pltpu.make_async_copy(dst, dst, sem).wait()

    fetch = [
        pltpu.make_async_copy(src, raw.at[n], in_sem.at[n]) for n, src in enumerate((k_hbm, v_hbm, q_hbm))
    ]
    fetch.append(pltpu.make_async_copy(bias_hbm, bias_ref, in_sem.at[3]))
    fetch.append(pltpu.make_async_copy(mask_hbm, mask, in_sem.at[4]))
    for cp in fetch:
        cp.start()
    barrier = pltpu.get_barrier_semaphore()
    for n in range(1, 64):
        pl.semaphore_signal(
            barrier, inc=1, device_id=(((a_me + n // 16) % 4) * 4 + x, (g + n) % 16), device_id_type=MESH
        )
    for dev in (left, right):
        pl.semaphore_signal(barrier, inc=1, device_id=dev, device_id_type=MESH)

    lane16 = lax.broadcasted_iota(jnp.int32, (16, 128), 1) < HD

    def prepare(t):
        fetch[t].wait()

        def body(p, carry):
            both = raw[t, :, pl.ds(pl.multiple_of(p * 128, 128), 128)].astype(F32)
            turned = pltpu.roll(both, HD, 1)
            sendbuf[t * 48 + 2 * p] = jnp.where(lane16, both[0:16], turned[16:32]).astype(BF16)
            sendbuf[t * 48 + 2 * p + 1] = jnp.where(lane16, turned[0:16], both[16:32]).astype(BF16)
            return carry

        lax.fori_loop(0, 24, body, 0, unroll=4)

    prepare(0)
    pl.semaphore_wait(barrier, 65)

    def send_wave(t, target):
        def body(n, carry):
            h = (n + 3 * g) % 48
            gd, kd = h // 3, h % 3
            ad = ((gd // 2) % 4 + 1 + kd) % 4
            here = (ad == a_me) & (gd == g)
            src = sendbuf.at[t * 48 + h]

            @pl.when(jnp.logical_not(here))
            def _():
                remote(src, target, e_send, e_recv.at[t, a_me], (ad * 4 + x, gd)).start()

            @pl.when(here)
            def _():
                pltpu.make_async_copy(src, target, e_recv.at[t, a_me]).start()

            return carry

        lax.fori_loop(0, 48, body, 0)

    def w1_copy(dx, r):
        yd, xx = (y + r) % 4, (x + dx) % 4
        rows = pl.ds(pl.multiple_of(xx * 48, 16), 48)
        return remote(
            w_hbm.at[rows, pl.ds(pl.multiple_of(yd * 768, 128), 768)], wbuf.at[y, zh, rows],
            w1_send.at[dx, r - 1], w1_recv.at[dx, r - 1], (seq, zh * 8 + yd * 2 + c),
        )

    w1_own = pltpu.make_async_copy(
        w_hbm.at[:, pl.ds(pl.multiple_of(y * 768, 128), 768)], wbuf.at[y, zh], w1_loc
    )
    w1_own.start()
    send_wave(0, kbuf.at[0, a_me, g])
    for r in range(1, 4):
        w1_copy(0, r).start()
    prepare(1)
    send_wave(1, vbuf.at[0, a_me, g])
    prepare(2)
    send_wave(2, qbuf.at[a_me, g])
    fetch[3].wait()
    fetch[4].wait()

    def x_copy(direction, t, a):
        buf = (kbuf, vbuf)[t]
        return remote(
            buf.at[0, a], buf.at[1 + direction, a],
            x_send.at[direction, t, a], x_recv.at[direction, t, a], (right, left)[direction],
        )

    def fk_copy(a):
        direction = a // 2
        return remote(
            kbuf.at[1 + direction, a], kbuf.at[3, a], fk_send.at[a], fk_recv.at[a], (right, left)[direction]
        )

    def fv_copy(direction, a):
        rows = pl.ds(8 * direction, 8)
        return remote(
            vbuf.at[1 + direction, a, rows], vbuf.at[3, a, rows],
            fv_send.at[direction, a], fv_recv.at[direction, a], (right, left)[direction],
        )

    def send_values(a):
        x_copy(0, 1, a).start()
        x_copy(1, 1, a).start()

    def pass_values(a):
        for direction in range(2):
            x_copy(direction, 1, a).wait_recv()
            fv_copy(direction, a).start()

    def got_values(a):
        fv_copy(0, a).wait_recv()
        fv_copy(1, a).wait_recv()

    half_lane = lax.broadcasted_iota(jnp.int32, (8, 128), 1) < HD

    def tile_rows(n, carry):
        midx, i = n // 4, n % 4
        for jt in range(2):
            one = jnp.where(mask[i, 2 * jt, midx] > 0, 0.0, NEG).astype(F32)
            two = jnp.where(mask[i, 2 * jt + 1, midx] > 0, 0.0, NEG).astype(F32)
            tiles[midx, i, jt] = jnp.where(half_lane, one, two)
        return carry

    @pl.when(active)
    def _():
        lax.fori_loop(0, 36, tile_rows, 0)
        tiles[9] = jnp.full((4, 2, 8, 128), NEG, F32)
        for a in (0, 2, 1, 3):
            arrived(kbuf.at[0, a], e_recv.at[0, a])
            x_copy(0, 0, a).start()
            x_copy(1, 0, a).start()
        for a in range(4):
            arrived(vbuf.at[0, a], e_recv.at[1, a])
            send_values(a)

    lane256 = lax.broadcasted_iota(jnp.int32, (256, 128), 1) < HD

    def value_sides(buf, ap):
        both = vbuf[buf, ap].astype(F32).reshape(256, 128)
        turned = pltpu.roll(both, HD, 1)
        lo = [jnp.where(lane256, v, 1.0).astype(BF16) for v in (both, turned)]
        hi = [jnp.where(lane256, 1.0, v).astype(BF16) for v in (turned, both)]
        return jnp.concatenate(lo, axis=0), jnp.concatenate(hi, axis=0)

    my_rows = pl.ds(pl.multiple_of(x * 48, 16), 48)

    def w2_copy(n):
        ref = wbuf.at[pl.ds(2 * n, 2), zh, my_rows]
        dev = ((3 - a_me) * 4 + x, other * 8 + y * 2 + c)
        return remote(ref, ref, w2_send.at[n], w2_recv.at[n], dev)

    def w2f_copy(n):
        ref = wbuf.at[pl.ds(2 * n, 2), other, my_rows]
        return remote(ref, ref, w2f_send.at[n], w2_recv.at[n], ((1 + a_me // 3) * 4 + x, g))

    def w3_copy(direction):
        ref = wbuf.at[:, other, my_rows]
        return remote(ref, ref, w3_send.at[direction], w3_recv.at[direction], (right, left)[direction])

    def w3f_copy(direction):
        xx = (x + (3, 1)[direction]) % 4
        ref = wbuf.at[pl.ds(2 * direction, 2), other, pl.ds(pl.multiple_of(xx * 48, 16), 48)]
        return remote(ref, ref, w3f_send.at[direction], w3f_recv.at[direction], (right, left)[direction])

    def w2_forward(n):
        @pl.when(boundary)
        def _():
            w2_copy(n).wait_recv()
            w2f_copy(n).start()

    @pl.when(jnp.logical_not(active))
    def _():
        arrived(sendbuf, e_send)

    for r in range(1, 4):
        w1_copy(0, r).wait()
    w1_own.wait()

    @pl.when(boundary)
    def _():
        w2_copy(0).start()
        w2_copy(1).start()

    @pl.when(active)
    def _():
        for a in (0, 2, 1, 3):
            x_copy(a // 2, 0, a).wait_recv()
            fk_copy(a).start()
        for a in range(4):
            sides[a, 0], sides[a, 1] = value_sides(0, a)
        for a in range(4):
            arrived(qbuf.at[a], e_recv.at[2, a])
            both = qbuf[a].astype(F32).reshape(256, 128)
            lo = jnp.where(lane256, both, 0.0)
            hi = jnp.where(lane256, 0.0, both)
            qlo[a, 0:256] = lo.astype(BF16)
            qlo[a, 256:512] = pltpu.roll(hi, HD, 1).astype(BF16)
            qhi[a, 0:256] = pltpu.roll(lo, HD, 1).astype(BF16)
            qhi[a, 256:512] = hi.astype(BF16)

    for dx in range(1, 4):
        for r in range(1, 4):
            w1_copy(dx, r).start()

    def update(a, blocks, first):
        scores = []
        for buf, ap, _ in blocks:
            keys = kbuf[buf, ap].reshape(256, 128)
            for q in (qlo, qhi):
                scores.append(
                    lax.dot_general(q[a], keys, (((1,), (1,)), ((), ())), preferred_element_type=F32)
                )
        weights = []
        alphas = []
        for n in range(8):
            rows = slice(n * 64, (n + 1) * 64)
            cols = []
            for b, (_, _, midx) in enumerate(blocks):
                for half in range(2):
                    for jt in range(2):
                        hide = tiles[midx, n % 4, jt][None]
                        tile = scores[2 * b + half][rows, jt * 128:(jt + 1) * 128]
                        cols.append((tile.reshape(8, 8, 128) + hide).reshape(64, 128))
            top = jnp.max(functools.reduce(jnp.maximum, cols), axis=1, keepdims=True)
            if first:
                m_new = jnp.broadcast_to(top, (64, 128))
            else:
                m_old = m_ref[a, rows]
                m_new = jnp.maximum(m_old, top)
                alphas.append(jnp.exp2((m_old - m_new) * SCALE2))
            m_ref[a, rows] = m_new
            weights.append(
                jnp.concatenate([jnp.exp2((tile - m_new) * SCALE2).astype(BF16) for tile in cols], axis=1)
            )
        values = [sides[ap] if first else value_sides(buf, ap) for buf, ap, _ in blocks]
        for half in range(2):
            rows = slice(half * 256, (half + 1) * 256)
            left_side = jnp.concatenate(weights[4 * half:4 * half + 4], axis=0)
            right_side = jnp.concatenate([v[half] for v in values], axis=0)
            new = jnp.dot(left_side, right_side, preferred_element_type=F32)
            if not first:
                new = acc_ref[a, rows] * jnp.concatenate(alphas[4 * half:4 * half + 4], axis=0) + new
            acc_ref[a, rows] = new

    def local(a):
        blocks = []
        for ap in range(4):
            off = ap - a
            midx = jnp.where(off > 0, 4 + 2 * off, 3 - 2 * off)
            midx = jnp.where(off == 0, 0, midx)
            blocks.append((0, ap, jnp.where((off > 2) | (off < -2), 9, midx)))
        update(a, blocks, True)

    def pair(buf_minus, buf_plus, step_minus, step_plus, midx):
        def body(a):
            minus, plus = a - step_minus, a + step_plus
            update(
                a,
                [
                    (buf_minus, jnp.maximum(minus, 0), jnp.where(minus >= 0, midx, 9)),
                    (buf_plus, jnp.minimum(plus, 3), jnp.where(plus <= 3, midx + 1, 9)),
                ],
                False,
            )

        return body

    near = pair(1, 2, (3 - x) // 3, (x + 1) // 4, 1)
    far = pair(3, 3, (3 - x) // 2, (x + 2) // 4, 3)

    def hand_over(a):
        lo, hi = acc_ref[a, 0:256], acc_ref[a, 256:512]
        total = pltpu.roll(jnp.where(lane256, hi, lo), HD, 1)
        packed = (jnp.where(lane256, lo, hi) / total).astype(BF16)
        slot = zh * 3 + k_me
        for hd in range(2):
            opack[2 * a + hd] = packed[hd * 128:(hd + 1) * 128]
            here = (a_me == a) & (zh == hd)
            src, dst = opack.at[2 * a + hd], attended.at[0, slot]

            @pl.when(jnp.logical_not(here))
            def _():
                remote(src, dst, o_send, o_recv.at[slot], (a * 4 + x, hd * 8 + y * 2 + c)).start()

            @pl.when(here)
            def _():
                pltpu.make_async_copy(src, dst, o_recv.at[slot]).start()

    def w3_begin():
        @pl.when(jnp.logical_not(boundary))
        def _():
            w2_copy(0).wait_recv()
            w2_copy(1).wait_recv()

        w3_copy(0).start()
        w3_copy(1).start()

    def local_pass(a, carry):
        local(a)
        for b in range(4):

            @pl.when(a == b)
            def _():
                pass_values(b)
                if b in (0, 2):
                    w2_forward(b // 2)

        return carry

    def near_pass(a, carry):
        near(a)
        return carry

    def far_pass(n, carry):
        a = (a_me + 4 - n) % 4
        far(a)
        hand_over(a)
        return carry

    @pl.when(active)
    def _():
        lax.fori_loop(0, 4, local_pass, 0)
        for a in range(4):
            x_copy(1 - a // 2, 0, a).wait_recv()
        lax.fori_loop(0, 4, near_pass, 0)
        for a in range(4):
            fk_copy(a).wait_recv()
            got_values(a)
        w3_begin()
        lax.fori_loop(0, 4, far_pass, 0)

    @pl.when(jnp.logical_not(active))
    def _():
        w2_forward(0)
        w2_forward(1)
        w3_begin()

    def a_copy(r, slot, h):
        rows = pl.ds(64 * h, 64)
        return remote(
            attended.at[0, slot, rows], attended.at[r, slot, rows],
            a_send.at[r - 1, slot, h], a_recv.at[r - 1, slot, h], (seq, zh * 8 + ((y + r) % 4) * 2 + c),
        )

    def gather(step, h):
        zs = (zh * 4 + a_me + step) % 8
        k = (zs % 4 + 7 - y) % 4
        slot = zs // 4 * 3 + k

        @pl.when(k < 3)
        def _():
            if h == 0:
                arrived(attended.at[0, slot], o_recv.at[slot])
            for r in (2, 1, 3):
                a_copy(r, slot, h).start()

    def w3_forward():
        for direction in range(2):
            w3_copy(direction).wait_recv()
            w3f_copy(direction).start()

    for n, step in enumerate(STEPS):
        gather(step, 0)
        if n >= LAG:
            gather(STEPS[n - LAG], 1)
    for step in STEPS[8 - LAG:]:
        gather(step, 1)
    w3_forward()

    lane64 = lax.broadcasted_iota(jnp.int32, (64, 128), 1) < HD

    def unpack(r, h):
        for t in range(3):
            x0 = attended[r, 2 * t, 64 * h:64 * h + 64].astype(F32)
            x1 = attended[r, 2 * t + 1, 64 * h:64 * h + 64].astype(F32)
            cols = slice(r * 384 + t * 128, r * 384 + (t + 1) * 128)
            lo = jnp.where(lane64, x0, pltpu.roll(x1, HD, 1)).astype(BF16).reshape(2, 2, 16, 128)
            hi = jnp.where(lane64, pltpu.roll(x0, HD, 1), x1).astype(BF16).reshape(2, 2, 16, 128)
            for cd in range(2):
                lhs[h, cd, :, 0, :, cols] = lo[:, cd]
                lhs[h, cd, :, 1, :, cols] = hi[:, cd]

    owners = (y, (y + 3) % 4, (y + 2) % 4, (y + 1) % 4)

    def project(h, n):
        rows = lhs[h].reshape(128, 1536)
        res = None
        for r in range(4):
            rhs = wbuf[owners[r], :, :, n * 256:(n + 1) * 256].reshape(384, 256)
            d = jnp.dot(rows[:, r * 384:(r + 1) * 384], rhs, preferred_element_type=F32)
            res = d if res is None else res + d
        part[h, n] = res.reshape(2, 64, 256)

    def d_copy(h, n):
        return remote(
            part.at[h, n, 1 - c], dpart.at[h, n], d_send.at[h, n], d_recv.at[h, n], (seq, g + 1 - 2 * c)
        )

    def y_cols(n):
        return pl.ds(pl.multiple_of(y * 768 + n * 256, 128), 256)

    def y_copy(yd, n, r):
        return remote(
            fin.at[yd, n], o_ref.at[:, y_cols(n)], y_send.at[yd, n], y_recv.at[r, n],
            (seq, zh * 8 + yd * 2 + c),
        )

    def begin_half(h):
        for r in (1, 3, 2):
            for slot in range(6):
                a_copy(r, slot, h).wait_recv()
            unpack(r, h)
        if h == 0:
            for direction in range(2):
                w3f_copy(direction).wait_recv()
            for dx in range(1, 4):
                for r in range(1, 4):
                    w1_copy(dx, r).wait()
        for n in range(3):
            project(h, n)
            d_copy(h, n).start()

    def end_half(h):
        for n in range(3):
            d_copy(h, n).wait_recv()
            bias = bias_ref[y_cols(n)].astype(F32)[None]
            done = (part[h, n, c] + dpart[h, n] + bias).astype(BF16).reshape(2, 32, 256)
            for b in range(2):
                yd = 2 * h + b
                fin[yd, n] = done[b]

                @pl.when(y != yd)
                def _():
                    y_copy(yd, n, (yd + 4 - y) % 4).start()

                @pl.when(y == yd)
                def _():
                    o_ref[:, y_cols(n)] = done[b]

    unpack(0, 0)
    unpack(0, 1)
    begin_half(0)

    @pl.when(active)
    def _():
        arrived(sendbuf.at[pl.ds(0, 141)], e_send)
        for t in range(2):
            for a in range(4):
                x_copy(0, t, a).wait_send()
                x_copy(1, t, a).wait_send()
        for a in range(4):
            fk_copy(a).wait_send()
            fv_copy(0, a).wait_send()
            fv_copy(1, a).wait_send()
        arrived(opack.at[pl.ds(0, 7)], o_send)

    @pl.when(boundary)
    def _():
        for n in range(2):
            w2_copy(n).wait_send()
            w2f_copy(n).wait_send()

    for direction in range(2):
        w3_copy(direction).wait_send()
        w3f_copy(direction).wait_send()

    end_half(0)
    begin_half(1)
    for r in range(1, 4):
        for slot in range(6):
            for h in range(2):
                a_copy(r, slot, h).wait_send()
    end_half(1)

    for n in range(3):
        for h in range(2):
            d_copy(h, n).wait_send()
        for yd in range(4):

            @pl.when(y != yd)
            def _():
                y_copy(yd, n, 0).wait_send()

        for r in range(1, 4):
            y_copy(0, n, r).wait_recv()


def shards(query_in, key_in, value_in, block_mask, out_weight, out_bias):
    hbm = pl.BlockSpec(memory_space=pltpu.HBM)
    dma = pltpu.SemaphoreType.DMA
    return pl.pallas_call(
        kernel,
        out_shape=jax.ShapeDtypeStruct((32, 3072), BF16),
        in_specs=[hbm] * 6,
        out_specs=pl.BlockSpec(memory_space=pltpu.VMEM),
        scratch_shapes=[
            pltpu.VMEM((3, 32, 3072), BF16),
            pltpu.SMEM((4, 4, 9), jnp.int32),
            pltpu.VMEM((3072,), BF16),
            pltpu.VMEM((144, 16, 128), BF16),
            pltpu.VMEM((4, 4, 16, 16, 128), BF16),
            pltpu.VMEM((4, 4, 16, 16, 128), BF16),
            pltpu.VMEM((4, 16, 16, 128), BF16),
            pltpu.VMEM((4, 512, 128), BF16),
            pltpu.VMEM((4, 512, 128), BF16),
            pltpu.VMEM((10, 4, 2, 8, 128), F32),
            pltpu.VMEM((4, 2, 512, 128), BF16),
            pltpu.VMEM((4, 512, 128), F32),
            pltpu.VMEM((4, 512, 128), F32),
            pltpu.VMEM((8, 128, 128), BF16),
            pltpu.VMEM((4, 6, 128, 128), BF16),
            pltpu.VMEM((2, 2, 2, 2, 16, 1536), BF16),
            pltpu.VMEM((4, 2, 192, 768), BF16),
            pltpu.VMEM((2, 3, 2, 64, 256), F32),
            pltpu.VMEM((2, 3, 64, 256), F32),
            pltpu.VMEM((4, 3, 32, 256), BF16),
            dma((5,)), dma, dma((3, 4)), dma((2, 2, 4)), dma((2, 2, 4)), dma((4,)), dma((4,)), dma((2, 4)), dma((2, 4)),
            dma((4, 3)), dma((4, 3)), dma, dma((2,)), dma((2,)), dma((2,)), dma((2,)), dma((2,)), dma((2,)), dma((2,)),
            dma, dma((6,)), dma((3, 6, 2)), dma((3, 6, 2)),
            dma((2, 3)), dma((2, 3)), dma((4, 3)), dma((4, 3)),
        ],
        compiler_params=pltpu.CompilerParams(
            collective_id=0, has_side_effects=True, vmem_limit_bytes=63 * 1024 * 1024
        ),
        name="radial",
    )(query_in, key_in, value_in, jnp.transpose(block_mask, (1, 2, 0)), out_weight, out_bias)


def solution(mesh):
    return jax.shard_map(
        shards,
        mesh=mesh,
        in_specs=(
            P(("seq", "head"), None),
            P(("seq", "head"), None),
            P(("seq", "head"), None),
            P(),
            P("head", None),
            P(),
        ),
        out_specs=P(("seq", "head"), None),
        check_vma=False,
    )
```

```python
import functools
import math

import jax
import jax.numpy as jnp
from jax import lax
from jax.experimental import pallas as pl
from jax.experimental.pallas import tpu as pltpu
from jax.sharding import PartitionSpec as P

MESH = pl.DeviceIdType.MESH
F32 = jnp.float32
BF16 = jnp.bfloat16
HD = 64
NEG = -1e30
STEPS = (0, 4, 1, 5, 2, 6, 3, 7)
LAG = 8
SCALE2 = math.log2(math.e) / math.sqrt(HD)


def kernel(
    q_hbm, k_hbm, v_hbm, mask_hbm, w_hbm, bias_hbm, o_ref,
    raw, mask, bias_ref, sendbuf, kbuf, vbuf, qbuf, qlo, qhi, tiles, sides, m_ref, acc_ref, opack,
    attended, lhs, wbuf, part, dpart, fin,
    in_sem, e_send, e_recv, x_send, x_recv, fk_send, fk_recv, fv_send, fv_recv,
    w1_send, w1_recv, w1_loc, w2_send, w2_recv, w2f_send, w3_send, w3_recv, w3f_send, w3f_recv,
    o_send, o_recv, a_send, a_recv, d_send, d_recv, y_send, y_recv,
):
    seq = lax.axis_index("seq")
    g = lax.axis_index("head")
    a_me, x = seq // 4, seq % 4
    zh, y, c = g // 8, (g // 2) % 4, g % 2
    k_me = (a_me + 3 - y) % 4
    active = k_me < 3
    boundary = (a_me % 3) == 0
    right = (a_me * 4 + (x + 1) % 4, g)
    left = (a_me * 4 + (x + 3) % 4, g)
    other = 1 - zh

    def remote(src, dst, send, rcv, dev):
        return pltpu.make_async_remote_copy(
            src_ref=src, dst_ref=dst, send_sem=send, recv_sem=rcv, device_id=dev, device_id_type=MESH
        )

    def arrived(dst, sem):
        pltpu.make_async_copy(dst, dst, sem).wait()

    fetch = [
        pltpu.make_async_copy(src, raw.at[n], in_sem.at[n]) for n, src in enumerate((k_hbm, v_hbm, q_hbm))
    ]
    fetch.append(pltpu.make_async_copy(bias_hbm, bias_ref, in_sem.at[3]))
    fetch.append(pltpu.make_async_copy(mask_hbm, mask, in_sem.at[4]))
    for cp in fetch:
        cp.start()
    barrier = pltpu.get_barrier_semaphore()
    for n in range(1, 64):
        pl.semaphore_signal(
            barrier, inc=1, device_id=(((a_me + n // 16) % 4) * 4 + x, (g + n) % 16), device_id_type=MESH
        )
    for dev in (left, right):
        pl.semaphore_signal(barrier, inc=1, device_id=dev, device_id_type=MESH)

    lane16 = lax.broadcasted_iota(jnp.int32, (16, 128), 1) < HD

    def prepare(t):
        fetch[t].wait()

        def body(p, carry):
            both = raw[t, :, pl.ds(pl.multiple_of(p * 128, 128), 128)].astype(F32)
            turned = pltpu.roll(both, HD, 1)
            sendbuf[t * 48 + 2 * p] = jnp.where(lane16, both[0:16], turned[16:32]).astype(BF16)
            sendbuf[t * 48 + 2 * p + 1] = jnp.where(lane16, turned[0:16], both[16:32]).astype(BF16)
            return carry

        lax.fori_loop(0, 24, body, 0, unroll=4)

    prepare(0)
    pl.semaphore_wait(barrier, 65)

    def send_wave(t, target):
        def body(n, carry):
            h = (n + 3 * g) % 48
            gd, kd = h // 3, h % 3
            ad = ((gd // 2) % 4 + 1 + kd) % 4
            here = (ad == a_me) & (gd == g)
            src = sendbuf.at[t * 48 + h]

            @pl.when(jnp.logical_not(here))
            def _():
                remote(src, target, e_send, e_recv.at[t, a_me], (ad * 4 + x, gd)).start()

            @pl.when(here)
            def _():
                pltpu.make_async_copy(src, target, e_recv.at[t, a_me]).start()

            return carry

        lax.fori_loop(0, 48, body, 0)

    def w1_copy(dx, r):
        yd, xx = (y + r) % 4, (x + dx) % 4
        rows = pl.ds(pl.multiple_of(xx * 48, 16), 48)
        return remote(
            w_hbm.at[rows, pl.ds(pl.multiple_of(yd * 768, 128), 768)], wbuf.at[y, zh, rows],
            w1_send.at[dx, r - 1], w1_recv.at[dx, r - 1], (seq, zh * 8 + yd * 2 + c),
        )

    w1_own = pltpu.make_async_copy(
        w_hbm.at[:, pl.ds(pl.multiple_of(y * 768, 128), 768)], wbuf.at[y, zh], w1_loc
    )
    w1_own.start()
    send_wave(0, kbuf.at[0, a_me, g])
    for r in range(1, 4):
        w1_copy(0, r).start()
    prepare(1)
    send_wave(1, vbuf.at[0, a_me, g])
    prepare(2)
    send_wave(2, qbuf.at[a_me, g])
    fetch[3].wait()
    fetch[4].wait()

    def x_copy(direction, t, a):
        buf = (kbuf, vbuf)[t]
        return remote(
            buf.at[0, a], buf.at[1 + direction, a],
            x_send.at[direction, t, a], x_recv.at[direction, t, a], (right, left)[direction],
        )

    def fk_copy(a):
        direction = a // 2
        return remote(
            kbuf.at[1 + direction, a], kbuf.at[3, a], fk_send.at[a], fk_recv.at[a], (right, left)[direction]
        )

    def fv_copy(direction, a):
        rows = pl.ds(8 * direction, 8)
        return remote(
            vbuf.at[1 + direction, a, rows], vbuf.at[3, a, rows],
            fv_send.at[direction, a], fv_recv.at[direction, a], (right, left)[direction],
        )

    def send_values(a):
        x_copy(0, 1, a).start()
        x_copy(1, 1, a).start()

    def pass_values(a):
        for direction in range(2):
            x_copy(direction, 1, a).wait_recv()
            fv_copy(direction, a).start()

    def got_values(a):
        fv_copy(0, a).wait_recv()
        fv_copy(1, a).wait_recv()

    half_lane = lax.broadcasted_iota(jnp.int32, (8, 128), 1) < HD

    def tile_rows(n, carry):
        midx, i = n // 4, n % 4
        for jt in range(2):
            one = jnp.where(mask[i, 2 * jt, midx] > 0, 0.0, NEG).astype(F32)
            two = jnp.where(mask[i, 2 * jt + 1, midx] > 0, 0.0, NEG).astype(F32)
            tiles[midx, i, jt] = jnp.where(half_lane, one, two)
        return carry

    @pl.when(active)
    def _():
        lax.fori_loop(0, 36, tile_rows, 0)
        tiles[9] = jnp.full((4, 2, 8, 128), NEG, F32)
        for a in (0, 2, 1, 3):
            arrived(kbuf.at[0, a], e_recv.at[0, a])
            x_copy(0, 0, a).start()
            x_copy(1, 0, a).start()
        for a in range(4):
            arrived(vbuf.at[0, a], e_recv.at[1, a])
            send_values(a)

    lane256 = lax.broadcasted_iota(jnp.int32, (256, 128), 1) < HD

    def value_sides(buf, ap):
        both = vbuf[buf, ap].astype(F32).reshape(256, 128)
        turned = pltpu.roll(both, HD, 1)
        lo = [jnp.where(lane256, v, 1.0).astype(BF16) for v in (both, turned)]
        hi = [jnp.where(lane256, 1.0, v).astype(BF16) for v in (turned, both)]
        return jnp.concatenate(lo, axis=0), jnp.concatenate(hi, axis=0)

    my_rows = pl.ds(pl.multiple_of(x * 48, 16), 48)

    def w2_copy(n):
        ref = wbuf.at[pl.ds(2 * n, 2), zh, my_rows]
        dev = ((3 - a_me) * 4 + x, other * 8 + y * 2 + c)
        return remote(ref, ref, w2_send.at[n], w2_recv.at[n], dev)

    def w2f_copy(n):
        ref = wbuf.at[pl.ds(2 * n, 2), other, my_rows]
        return remote(ref, ref, w2f_send.at[n], w2_recv.at[n], ((1 + a_me // 3) * 4 + x, g))

    def w3_copy(direction):
        ref = wbuf.at[:, other, my_rows]
        return remote(ref, ref, w3_send.at[direction], w3_recv.at[direction], (right, left)[direction])

    def w3f_copy(direction):
        xx = (x + (3, 1)[direction]) % 4
        ref = wbuf.at[pl.ds(2 * direction, 2), other, pl.ds(pl.multiple_of(xx * 48, 16), 48)]
        return remote(ref, ref, w3f_send.at[direction], w3f_recv.at[direction], (right, left)[direction])

    def w2_forward(n):
        @pl.when(boundary)
        def _():
            w2_copy(n).wait_recv()
            w2f_copy(n).start()

    @pl.when(jnp.logical_not(active))
    def _():
        arrived(sendbuf, e_send)

    for r in range(1, 4):
        w1_copy(0, r).wait()
    w1_own.wait()

    @pl.when(boundary)
    def _():
        w2_copy(0).start()
        w2_copy(1).start()

    @pl.when(active)
    def _():
        for a in (0, 2, 1, 3):
            x_copy(a // 2, 0, a).wait_recv()
            fk_copy(a).start()
        for a in range(4):
            sides[a, 0], sides[a, 1] = value_sides(0, a)
        for a in range(4):
            arrived(qbuf.at[a], e_recv.at[2, a])
            both = qbuf[a].astype(F32).reshape(256, 128)
            lo = jnp.where(lane256, both, 0.0)
            hi = jnp.where(lane256, 0.0, both)
            qlo[a, 0:256] = lo.astype(BF16)
            qlo[a, 256:512] = pltpu.roll(hi, HD, 1).astype(BF16)
            qhi[a, 0:256] = pltpu.roll(lo, HD, 1).astype(BF16)
            qhi[a, 256:512] = hi.astype(BF16)

    for dx in range(1, 4):
        for r in range(1, 4):
            w1_copy(dx, r).start()

    def update(a, blocks, first):
        scores = []
        for buf, ap, _ in blocks:
            keys = kbuf[buf, ap].reshape(256, 128)
            for q in (qlo, qhi):
                scores.append(
                    lax.dot_general(q[a], keys, (((1,), (1,)), ((), ())), preferred_element_type=F32)
                )
        weights = []
        alphas = []
        for n in range(8):
            rows = slice(n * 64, (n + 1) * 64)
            cols = []
            for b, (_, _, midx) in enumerate(blocks):
                for half in range(2):
                    for jt in range(2):
                        hide = tiles[midx, n % 4, jt][None]
                        tile = scores[2 * b + half][rows, jt * 128:(jt + 1) * 128]
                        cols.append((tile.reshape(8, 8, 128) + hide).reshape(64, 128))
            top = jnp.max(functools.reduce(jnp.maximum, cols), axis=1, keepdims=True)
            if first:
                m_new = jnp.broadcast_to(top, (64, 128))
            else:
                m_old = m_ref[a, rows]
                m_new = jnp.maximum(m_old, top)
                alphas.append(jnp.exp2((m_old - m_new) * SCALE2))
            m_ref[a, rows] = m_new
            weights.append(
                jnp.concatenate([jnp.exp2((tile - m_new) * SCALE2).astype(BF16) for tile in cols], axis=1)
            )
        values = [sides[ap] if first else value_sides(buf, ap) for buf, ap, _ in blocks]
        for half in range(2):
            rows = slice(half * 256, (half + 1) * 256)
            left_side = jnp.concatenate(weights[4 * half:4 * half + 4], axis=0)
            right_side = jnp.concatenate([v[half] for v in values], axis=0)
            new = jnp.dot(left_side, right_side, preferred_element_type=F32)
            if not first:
                new = acc_ref[a, rows] * jnp.concatenate(alphas[4 * half:4 * half + 4], axis=0) + new
            acc_ref[a, rows] = new

    def local(a):
        def some(first, count):
            blocks = []
            for step in range(count):
                off = first + step - a
                midx = jnp.where(off > 0, 4 + 2 * off, 3 - 2 * off)
                blocks.append((0, first + step, jnp.where(off == 0, 0, midx)))
            update(a, blocks, True)

        outer = (a == 0) | (a == 3)

        @pl.when(outer)
        def _():
            some(a // 3, 3)

        @pl.when(jnp.logical_not(outer))
        def _():
            some(0, 4)

    def pair(buf_minus, buf_plus, step_minus, step_plus, midx):
        def body(a):
            minus, plus = a - step_minus, a + step_plus
            update(
                a,
                [
                    (buf_minus, jnp.maximum(minus, 0), jnp.where(minus >= 0, midx, 9)),
                    (buf_plus, jnp.minimum(plus, 3), jnp.where(plus <= 3, midx + 1, 9)),
                ],
                False,
            )

        return body

    near = pair(1, 2, (3 - x) // 3, (x + 1) // 4, 1)
    far = pair(3, 3, (3 - x) // 2, (x + 2) // 4, 3)

    def hand_over(a):
        lo, hi = acc_ref[a, 0:256], acc_ref[a, 256:512]
        total = pltpu.roll(jnp.where(lane256, hi, lo), HD, 1)
        packed = (jnp.where(lane256, lo, hi) / total).astype(BF16)
        slot = zh * 3 + k_me
        for hd in range(2):
            opack[2 * a + hd] = packed[hd * 128:(hd + 1) * 128]
            here = (a_me == a) & (zh == hd)
            src, dst = opack.at[2 * a + hd], attended.at[0, slot]

            @pl.when(jnp.logical_not(here))
            def _():
                remote(src, dst, o_send, o_recv.at[slot], (a * 4 + x, hd * 8 + y * 2 + c)).start()

            @pl.when(here)
            def _():
                pltpu.make_async_copy(src, dst, o_recv.at[slot]).start()

    def w3_begin():
        @pl.when(jnp.logical_not(boundary))
        def _():
            w2_copy(0).wait_recv()
            w2_copy(1).wait_recv()

        w3_copy(0).start()
        w3_copy(1).start()

    def local_pass(a, carry):
        local(a)
        for b in range(1, 4):

            @pl.when(a == b)
            def _():
                if b == 1:
                    pass_values(0)
                pass_values(b)
                if b < 3:
                    w2_forward(b - 1)

        return carry

    def near_pass(a, carry):
        near(a)
        return carry

    def far_pass(n, carry):
        a = (a_me + 4 - n) % 4
        far(a)
        hand_over(a)
        return carry

    @pl.when(active)
    def _():
        lax.fori_loop(0, 4, local_pass, 0)
        for a in range(4):
            x_copy(1 - a // 2, 0, a).wait_recv()
        lax.fori_loop(0, 4, near_pass, 0)
        for a in range(4):
            fk_copy(a).wait_recv()
            got_values(a)
        w3_begin()
        lax.fori_loop(0, 4, far_pass, 0)

    @pl.when(jnp.logical_not(active))
    def _():
        w2_forward(0)
        w2_forward(1)
        w3_begin()

    def a_copy(r, slot, h):
        rows = pl.ds(64 * h, 64)
        return remote(
            attended.at[0, slot, rows], attended.at[r, slot, rows],
            a_send.at[r - 1, slot, h], a_recv.at[r - 1, slot, h], (seq, zh * 8 + ((y + r) % 4) * 2 + c),
        )

    def gather(step, h):
        zs = (zh * 4 + a_me + step) % 8
        k = (zs % 4 + 7 - y) % 4
        slot = zs // 4 * 3 + k

        @pl.when(k < 3)
        def _():
            if h == 0:
                arrived(attended.at[0, slot], o_recv.at[slot])
            for r in (2, 1, 3):
                a_copy(r, slot, h).start()

    def w3_forward():
        for direction in range(2):
            w3_copy(direction).wait_recv()
            w3f_copy(direction).start()

    for n, step in enumerate(STEPS):
        gather(step, 0)
        if n >= LAG:
            gather(STEPS[n - LAG], 1)
    for step in STEPS[8 - LAG:]:
        gather(step, 1)
    w3_forward()

    lane64 = lax.broadcasted_iota(jnp.int32, (64, 128), 1) < HD

    def unpack(r, h):
        for t in range(3):
            x0 = attended[r, 2 * t, 64 * h:64 * h + 64].astype(F32)
            x1 = attended[r, 2 * t + 1, 64 * h:64 * h + 64].astype(F32)
            cols = slice(r * 384 + t * 128, r * 384 + (t + 1) * 128)
            lo = jnp.where(lane64, x0, pltpu.roll(x1, HD, 1)).astype(BF16).reshape(2, 2, 16, 128)
            hi = jnp.where(lane64, pltpu.roll(x0, HD, 1), x1).astype(BF16).reshape(2, 2, 16, 128)
            for cd in range(2):
                lhs[h, cd, :, 0, :, cols] = lo[:, cd]
                lhs[h, cd, :, 1, :, cols] = hi[:, cd]

    owners = (y, (y + 3) % 4, (y + 2) % 4, (y + 1) % 4)

    def project(h, n):
        rows = lhs[h].reshape(128, 1536)
        res = None
        for r in range(4):
            rhs = wbuf[owners[r], :, :, n * 256:(n + 1) * 256].reshape(384, 256)
            d = jnp.dot(rows[:, r * 384:(r + 1) * 384], rhs, preferred_element_type=F32)
            res = d if res is None else res + d
        part[h, n] = res.reshape(2, 64, 256)

    def d_copy(h, n):
        return remote(
            part.at[h, n, 1 - c], dpart.at[h, n], d_send.at[h, n], d_recv.at[h, n], (seq, g + 1 - 2 * c)
        )

    def y_cols(n):
        return pl.ds(pl.multiple_of(y * 768 + n * 256, 128), 256)

    def y_copy(yd, n, r):
        return remote(
            fin.at[yd, n], o_ref.at[:, y_cols(n)], y_send.at[yd, n], y_recv.at[r, n],
            (seq, zh * 8 + yd * 2 + c),
        )

    def begin_half(h):
        for r in (1, 3, 2):
            for slot in range(6):
                a_copy(r, slot, h).wait_recv()
            unpack(r, h)
        if h == 0:
            for direction in range(2):
                w3f_copy(direction).wait_recv()
            for dx in range(1, 4):
                for r in range(1, 4):
                    w1_copy(dx, r).wait()
        for n in range(3):
            project(h, n)
            d_copy(h, n).start()

    def end_half(h):
        for n in range(3):
            d_copy(h, n).wait_recv()
            bias = bias_ref[y_cols(n)].astype(F32)[None]
            done = (part[h, n, c] + dpart[h, n] + bias).astype(BF16).reshape(2, 32, 256)
            for b in range(2):
                yd = 2 * h + b
                fin[yd, n] = done[b]

                @pl.when(y != yd)
                def _():
                    y_copy(yd, n, (yd + 4 - y) % 4).start()

                @pl.when(y == yd)
                def _():
                    o_ref[:, y_cols(n)] = done[b]

    unpack(0, 0)
    unpack(0, 1)
    begin_half(0)

    @pl.when(active)
    def _():
        arrived(sendbuf.at[pl.ds(0, 141)], e_send)
        for t in range(2):
            for a in range(4):
                x_copy(0, t, a).wait_send()
                x_copy(1, t, a).wait_send()
        for a in range(4):
            fk_copy(a).wait_send()
            fv_copy(0, a).wait_send()
            fv_copy(1, a).wait_send()
        arrived(opack.at[pl.ds(0, 7)], o_send)

    @pl.when(boundary)
    def _():
        for n in range(2):
            w2_copy(n).wait_send()
            w2f_copy(n).wait_send()

    for direction in range(2):
        w3_copy(direction).wait_send()
        w3f_copy(direction).wait_send()

    end_half(0)
    begin_half(1)
    for r in range(1, 4):
        for slot in range(6):
            for h in range(2):
                a_copy(r, slot, h).wait_send()
    end_half(1)

    for n in range(3):
        for h in range(2):
            d_copy(h, n).wait_send()
        for yd in range(4):

            @pl.when(y != yd)
            def _():
                y_copy(yd, n, 0).wait_send()

        for r in range(1, 4):
            y_copy(0, n, r).wait_recv()


def shards(query_in, key_in, value_in, block_mask, out_weight, out_bias):
    hbm = pl.BlockSpec(memory_space=pltpu.HBM)
    dma = pltpu.SemaphoreType.DMA
    return pl.pallas_call(
        kernel,
        out_shape=jax.ShapeDtypeStruct((32, 3072), BF16),
        in_specs=[hbm] * 6,
        out_specs=pl.BlockSpec(memory_space=pltpu.VMEM),
        scratch_shapes=[
            pltpu.VMEM((3, 32, 3072), BF16),
            pltpu.SMEM((4, 4, 9), jnp.int32),
            pltpu.VMEM((3072,), BF16),
            pltpu.VMEM((144, 16, 128), BF16),
            pltpu.VMEM((4, 4, 16, 16, 128), BF16),
            pltpu.VMEM((4, 4, 16, 16, 128), BF16),
            pltpu.VMEM((4, 16, 16, 128), BF16),
            pltpu.VMEM((4, 512, 128), BF16),
            pltpu.VMEM((4, 512, 128), BF16),
            pltpu.VMEM((10, 4, 2, 8, 128), F32),
            pltpu.VMEM((4, 2, 512, 128), BF16),
            pltpu.VMEM((4, 512, 128), F32),
            pltpu.VMEM((4, 512, 128), F32),
            pltpu.VMEM((8, 128, 128), BF16),
            pltpu.VMEM((4, 6, 128, 128), BF16),
            pltpu.VMEM((2, 2, 2, 2, 16, 1536), BF16),
            pltpu.VMEM((4, 2, 192, 768), BF16),
            pltpu.VMEM((2, 3, 2, 64, 256), F32),
            pltpu.VMEM((2, 3, 64, 256), F32),
            pltpu.VMEM((4, 3, 32, 256), BF16),
            dma((5,)), dma, dma((3, 4)), dma((2, 2, 4)), dma((2, 2, 4)), dma((4,)), dma((4,)), dma((2, 4)), dma((2, 4)),
            dma((4, 3)), dma((4, 3)), dma, dma((2,)), dma((2,)), dma((2,)), dma((2,)), dma((2,)), dma((2,)), dma((2,)),
            dma, dma((6,)), dma((3, 6, 2)), dma((3, 6, 2)),
            dma((2, 3)), dma((2, 3)), dma((4, 3)), dma((4, 3)),
        ],
        compiler_params=pltpu.CompilerParams(
            collective_id=0, has_side_effects=True, vmem_limit_bytes=63 * 1024 * 1024
        ),
        name="radial",
    )(query_in, key_in, value_in, jnp.transpose(block_mask, (1, 2, 0)), out_weight, out_bias)


def solution(mesh):
    return jax.shard_map(
        shards,
        mesh=mesh,
        in_specs=(
            P(("seq", "head"), None),
            P(("seq", "head"), None),
            P(("seq", "head"), None),
            P(),
            P("head", None),
            P(),
        ),
        out_specs=P(("seq", "head"), None),
        check_vma=False,
    )
```
